256 devices in a mesh: lat: 32 (over z_hi, y, core), lon: 8 (over x, z_lo).
Axes of the slice: x: 4, y: 4, z: 8 (z_hi: 4, z_lo: 2; z = z_hi * 2 + z_lo), core: 2. Of those that a mesh axis runs over, the one named last changes fastest.
Arguments:
- grid_cot: float32 [4, 64, 16, 5120], P(None, 'lat', None, 'lon'), may hold values from -6 to 6
- weights: bfloat16 [64, 16, 4, 5120], P('lat', None, None, 'lon'), may hold values from 0 to 1
- offsets: int32 [64, 16, 2, 5120], P('lat', None, None, 'lon'), may hold values from -4 to 3, as said below
- lat_points: int32 [64], P('lat'), may hold values from 1280 to 5120
- slot_mode: int32 [1280], replicated, may hold values from 0 to 1279, each once
- legendre: bfloat16 [1280, 64, 1280], P('lat'), may hold values from -0.009765625 to 0.009765625
Outputs:
- spectral_cot: bfloat16 [1280, 2, 4, 16, 1280], P('lat', None, None, 'lon')
The draws below stay inside these ranges and needn't reach their ends.
Inputs may be any that keep to these rules, and one draw needn't show every extreme that they name: offsets[i, v, 0, j] is -1 or 0 and rows i + offsets[i, v, 0, j] and that plus 1 lie in the grid; offsets[i, v, 1, j] lies in -4 to 3. `slot_mode`: a permutation of the wavenumbers; the device with index k along lat owns slots k * 1280 / 32 onward.
All inputs are finite; a program needn't handle non-finite values.
Results may differ from the reference program's by a relative error of at most 0.005.
Values may be sent and summed in bfloat16 or wider, within the bound.
No kernel may reach another device: no remote copies, remote signals or barrier semaphores. Data moves between devices by JAX's collectives and lax.ppermute only.
A program may use at most 64 MiB of HBM per device.

```python
import jax
import jax.numpy as jnp
from jax import lax

FIELDS = 4
NLON = 5120
M = 1280
NL = 1280
REACH_LON = 4
LEV = 16
NLAT = 64
N_LAT = 32


def draw_offsets(key, part):
    key = jax.random.fold_in(key, 11)
    first_key, second_key = jax.random.split(key)
    layout = (NLAT, LEV, 1, NLON)
    row_index = lax.broadcasted_iota(jnp.int32, layout, 0)
    north_shift = jax.random.randint(first_key, layout, -1, 1)
    north_shift = jnp.where(row_index == 0, 0, north_shift)
    north_shift = jnp.where(row_index == NLAT - 1, -1, north_shift)
    east_shift = jax.random.randint(second_key, layout, -REACH_LON, REACH_LON)
    return jnp.concatenate([north_shift, east_shift], axis=2).astype(jnp.int32)


def place_ends(entries, rng, low, top_value):
    index_at = [jax.random.randint(jax.random.fold_in(rng, axis), (), 0, length) for axis, length in enumerate(entries.shape)]
    widest = entries.shape.index(max(entries.shape))
    next_to = index_at[:widest] + [(index_at[widest] + 1) % entries.shape[widest]] + index_at[widest + 1:]
    return entries.at[tuple(index_at)].set(low).at[tuple(next_to)].set(top_value)


def shard_levels(own_key, dims, cuts, least, top_value):
    def one(position, shards_of):
        steps = jax.random.uniform(jax.random.fold_in(jax.random.fold_in(own_key, 6), position), (shards_of,), jnp.float32, least / len(cuts), top_value / len(cuts))
        return jnp.repeat(jnp.exp(steps), dims[position] // shards_of).reshape((-1,) + (1,) * (len(dims) - position - 1))

    factor_of = one(*cuts[0])
    for cut in cuts[1:]:
        factor_of = factor_of * one(*cut)
    return factor_of


def gaussian(rng, shape, width, bound, pieces=(), kind=jnp.bfloat16):
    values = jax.random.normal(rng, shape, jnp.float32) * width
    if len(pieces) > 0:
        values = shard_levels(rng, shape, pieces, -0.22, 0.18) * values
    return jnp.clip(values, min=-bound, max=bound).astype(kind)


def setup_inputs(seed: int = 0) -> dict:
    key_list = jax.random.split(jax.random.key(seed), 7)
    grid_cot = gaussian(key_list[0], (FIELDS, NLAT, LEV, NLON), 1.0, 6.0, ((1, 32), (3, 8)), jnp.float32)
    weights = jnp.clip(1.0 * jax.random.uniform(key_list[1], (NLAT, LEV, 4, NLON), jnp.float32) ** shard_levels(key_list[1], (NLAT, LEV, 4, NLON), ((0, 32), (3, 8)), -0.2, 0.2), 0.0, 1.0).astype(jnp.bfloat16)
    offsets = draw_offsets(jax.random.fold_in(key_list[6], 71), 0)
    lat_points = place_ends(jax.random.randint(key_list[3], (NLAT,), NLON // 4, NLON + 1), jax.random.fold_in(key_list[3], 1), NLON // 4, NLON).astype(jnp.int32)
    slot_mode = jax.random.permutation(key_list[4], M).astype(jnp.int32)
    legendre = gaussian(key_list[5], (M, NLAT, NL), (NLAT * NLON) ** -0.5, 0.009765625, ((0, 32),))
    return {"grid_cot": grid_cot, "weights": weights, "offsets": offsets, "lat_points": lat_points, "slot_mode": slot_mode, "legendre": legendre}


def fourier_table(first_col, col_count, modes, circle):
    longitude = first_col + jnp.arange(col_count, dtype=jnp.int32)
    wavenumber = jnp.arange(modes, dtype=jnp.int32)
    phase = (longitude[:, None] * wavenumber[None, :]) % circle
    angle = (2.0 * jnp.pi / circle) * phase.astype(jnp.float32)
    factor = jnp.where(wavenumber == 0, 1.0, 2.0).astype(jnp.float32)
    return jnp.concatenate([factor * jnp.cos(angle), -factor * jnp.sin(angle)], axis=1)


def reference(grid_cot, weights, offsets, lat_points, slot_mode, legendre):
    fields, lat_count, levels, lon_count = grid_cot.shape
    row_index = jnp.arange(lat_count, dtype=jnp.int32)[:, None, None]
    level_index = jnp.arange(levels, dtype=jnp.int32)[None, :, None]
    col_index = jnp.arange(lon_count, dtype=jnp.int32)[None, None, :]
    deposit = jnp.zeros((fields, lat_count * levels * lon_count), jnp.float32)
    for north_step in range(2):
        for east_step in range(2):
            target_row = row_index + offsets[:, :, 0, :] + north_step
            target_col = (col_index + offsets[:, :, 1, :] + east_step) % lon_count
            flat_index = (target_row * levels + level_index) * lon_count + target_col
            weight_part = weights[:, :, 2 * north_step + east_step, :].astype(jnp.float32)
            deposit = deposit.at[:, flat_index].add(grid_cot * weight_part[None])
    deposit = deposit.reshape(fields, lat_count, levels, lon_count)
    fourier = fourier_table(0, lon_count, M, lon_count)
    spectra = jnp.dot(deposit, fourier, precision=lax.Precision.HIGHEST, preferred_element_type=jnp.float32)
    spectra = spectra.reshape(fields, lat_count, levels, 2, M)
    wavenumber = jnp.arange(M, dtype=jnp.int32)
    mode_mask = (2 * wavenumber[None, :] < lat_points[:, None]).astype(jnp.float32)
    masked = (spectra * mode_mask[None, :, None, None, :]).astype(jnp.bfloat16)
    ordered = jnp.take(masked, slot_mode, axis=4)
    per_block = M // N_LAT
    degree = jnp.arange(NL, dtype=jnp.int32)

    def one_block(block_index):
        first_slot = (block_index * per_block).astype(jnp.int32)
        table_block = lax.dynamic_slice_in_dim(legendre, first_slot, per_block, 0).astype(jnp.float32)
        coeff_block = lax.dynamic_slice_in_dim(ordered, first_slot, per_block, 4).astype(jnp.float32)
        modes_block = lax.dynamic_slice_in_dim(slot_mode, first_slot, per_block, 0)
        result = jnp.einsum('stl,ftvrs->srfvl', table_block, coeff_block, precision=lax.Precision.HIGHEST)
        degree_mask = (degree[None, :] >= modes_block[:, None]).astype(jnp.float32)
        return (result * degree_mask[:, None, None, None, :]).astype(jnp.bfloat16)

    blocks_out = lax.map(one_block, jnp.arange(N_LAT, dtype=jnp.int32))
    return blocks_out.reshape(M, 2, fields, levels, NL)
```

```python
import functools

import jax
import jax.numpy as jnp
import numpy as np
from jax import lax
from jax.experimental import pallas as pl
from jax.experimental.pallas import tpu as pltpu
from jax.sharding import PartitionSpec as P

FIELDS = 4
NLON = 5120
M = 1280
NL = 1280
REACH = 4
LEV = 16
ROWS = 2
TARGETS = ROWS + 2
SECTORS = 8
BANDS = 32
COLS = NLON // SECTORS
WIDE = 768
PER_PEER = LEV // SECTORS
LINES = TARGETS * FIELDS * PER_PEER
SLOTS = M // BANDS
LANE_SLOTS = 8
GROUPS = SLOTS // LANE_SLOTS
MSG = TARGETS * (GROUPS + 1)
NLAT = ROWS * BANDS
VMEM = 56 * 1024 * 1024

F32 = jnp.float32
BF16 = jnp.bfloat16


def dot(a, b, dims):
    return lax.dot_general(a, b, (dims, ((), ())), preferred_element_type=F32)


def level_order():
    order = np.zeros((FIELDS * TARGETS * LEV, FIELDS * TARGETS * LEV), np.float32)
    for peer in range(SECTORS):
        for t in range(TARGETS):
            for f in range(FIELDS):
                for v in range(PER_PEER):
                    out = ((peer * TARGETS + t) * FIELDS + f) * PER_PEER + v
                    order[out, (f * TARGETS + t) * LEV + peer * PER_PEER + v] = 1
    return order.astype(BF16)


def message_order():
    order = np.zeros((BANDS * MSG, TARGETS * BANDS * GROUPS), np.float32)
    for k in range(BANDS):
        for t in range(TARGETS):
            for g in range(GROUPS):
                order[k * MSG + t * (GROUPS + 1) + g, (t * BANDS + k) * GROUPS + g] = 1
    return order.astype(BF16)


def latitude_order():
    order = np.zeros((BANDS * MSG, (GROUPS + 1) * 2 * NLAT), np.float32)
    for k in range(BANDS):
        for t in range(TARGETS):
            i = ROWS * k + t - 1
            if 0 <= i < NLAT:
                for g in range(GROUPS + 1):
                    for twice in range(2):
                        order[k * MSG + t * (GROUPS + 1) + g, (g * 2 + twice) * NLAT + i] = 1
    return order.astype(BF16)


def deposit_kernel(grid_ref, weight_ref, offset_ref, order_ref, out_ref, coef, stacked):
    zeros = jnp.zeros((LEV, COLS), F32)
    for i in range(ROWS):
        offs = offset_ref[i]
        south = offs[:, 0, :] == -1
        east = offs[:, 1, :]
        wide_weights = weight_ref[i].astype(F32)
        w = [wide_weights[:, c, :] for c in range(4)]
        by_row = (
            [jnp.where(south, w[q], zeros) for q in range(2)],
            [jnp.where(south, w[2 + q], w[q]) for q in range(2)],
            [jnp.where(south, zeros, w[2 + q]) for q in range(2)],
        )
        for n, shift in enumerate(range(REACH, -REACH - 1, -1)):
            west_here = east == shift
            east_here = east == shift - 1
            for r in range(3):
                coef[n, i, r] = jnp.where(west_here, by_row[r][0], jnp.where(east_here, by_row[r][1], zeros))
    pad = jnp.zeros((8, WIDE - COLS), F32)
    for f in range(FIELDS):
        for half in range(LEV // 8):
            part = pl.ds(8 * half, 8)
            g = [grid_ref[f, i, part, :] for i in range(ROWS)]
            total = [None] * TARGETS
            for n in range(2 * REACH + 1):
                for t in range(TARGETS):
                    piece = None
                    for i in range(ROWS):
                        r = t - i
                        if 0 <= r < 3:
                            term = g[i] * coef[n, i, r, part, :]
                            piece = term if piece is None else piece + term
                    piece = jnp.concatenate([piece, pad], axis=1)
                    if n == 0:
                        total[t] = piece
                    else:
                        total[t] = pltpu.roll(total[t], 1, 1) + piece
            for t in range(TARGETS):
                stacked[pl.ds((f * TARGETS + t) * LEV + 8 * half, 8), :] = total[t]
    ordered = dot(order_ref[...], stacked[...].astype(BF16), ((1,), (0,)))
    out_ref[...] = ordered.astype(BF16).reshape(out_ref.shape)


def sincos(count):
    turn = count - NLON * jnp.round(count * (1.0 / NLON))
    quarter = jnp.round(turn * (4.0 / NLON))
    x = (turn - (NLON // 4) * quarter) * np.float32(2.0 * np.pi / NLON)
    y = x * x
    s = x * (1.0 + y * (-1.0 / 6 + y * (1.0 / 120 + y * (-1.0 / 5040 + y * (1.0 / 362880)))))
    c = 1.0 + y * (-1.0 / 2 + y * (1.0 / 24 + y * (-1.0 / 720 + y * (1.0 / 40320))))
    odd = jnp.abs(quarter) == 1.0
    cosine = jnp.where(odd, s, c)
    sine = jnp.where(odd, c, s)
    cosine = jnp.where((quarter == 1.0) | (jnp.abs(quarter) == 2.0), -cosine, cosine)
    sine = jnp.where((quarter == -1.0) | (jnp.abs(quarter) == 2.0), -sine, sine)
    return cosine, sine


STEP = 32


def table_kernel(mode_ref, table_ref, turn_ref):
    mode = mode_ref[...].astype(F32)

    def rows(count, scale, first):
        index = lax.broadcasted_iota(jnp.int32, (count, M), 0) * scale + first
        return sincos(index.astype(F32) * mode)

    coarse_c, coarse_s = rows(WIDE // STEP, STEP, 0)
    fine_c, fine_s = rows(STEP, 1, -REACH)
    factor = jnp.where(mode == 0.0, 1.0, 2.0)
    fine_c = fine_c * factor
    fine_s = fine_s * factor
    for a in range(WIDE // STEP):
        c = coarse_c[a : a + 1]
        s = coarse_s[a : a + 1]
        table_ref[a * STEP : (a + 1) * STEP, :M] = (c * fine_c - s * fine_s).astype(BF16)
        table_ref[a * STEP : (a + 1) * STEP, M:] = (-s * fine_c - c * fine_s).astype(BF16)
    turn_c, turn_s = rows(SECTORS, COLS, 0)
    turn_ref[0] = turn_c
    turn_ref[1] = turn_s


BLOCK = 256


def fourier_kernel(points_ref, grid_ref, table_ref, turn_ref, order_ref, out_ref, spectra, lanes):
    data = grid_ref[...].reshape(SECTORS * LINES, WIDE)
    for start in range(0, M, BLOCK):
        part = slice(start, start + BLOCK)
        real = dot(data, table_ref[:, part], ((1,), (0,)))
        imag = dot(data, table_ref[:, M + start : M + start + BLOCK], ((1,), (0,)))
        sum_r = jnp.zeros((LINES, BLOCK), F32)
        sum_i = jnp.zeros((LINES, BLOCK), F32)
        for j in range(SECTORS):
            c = turn_ref[0, j : j + 1, part]
            s = turn_ref[1, j : j + 1, part]
            re = real[j * LINES : (j + 1) * LINES]
            im = imag[j * LINES : (j + 1) * LINES]
            sum_r = sum_r + c * re + s * im
            sum_i = sum_i + c * im - s * re
        for t in range(TARGETS):
            rows = slice(8 * t, 8 * t + 8)
            spectra[t, :, part] = jnp.concatenate([sum_r[rows], sum_i[rows]], axis=0).astype(BF16)
    run = BANDS * GROUPS
    for t in range(TARGETS):
        for b in range(LANE_SLOTS):
            lanes[16 * b : 16 * b + 16, t * run : (t + 1) * run] = spectra[t, :, b * run : (b + 1) * run]
    message = dot(order_ref[...], lanes[...], ((1,), (1,)))
    row = lax.broadcasted_iota(jnp.int32, (MSG, 128), 0)
    lane = lax.broadcasted_iota(jnp.int32, (MSG, 128), 1)
    extra = jnp.zeros((MSG, 128), F32)
    for i in range(ROWS):
        count = (points_ref[i] + 1) // 2
        high = count // 16
        value = jnp.where(lane == 0, high, jnp.where(lane == 1, count - 16 * high, 0))
        extra = extra + jnp.where(row == (i + 1) * (GROUPS + 1) + GROUPS, value, 0).astype(F32)
    for k in range(BANDS):
        out_ref[k] = (message[k * MSG : (k + 1) * MSG] + extra).astype(BF16)


def legendre_kernel(mode_ref, band_ref, msg_ref, legendre_ref, order_ref, out_ref):
    base = band_ref[0] * SLOTS
    received = msg_ref[...].reshape(BANDS * MSG, 128)
    spread = dot(received, order_ref[...], ((0,), (0,)))
    lp = spread[:, GROUPS * 128 :]
    limit = 16.0 * lp[0:1] + lp[1:2]
    lane = lax.broadcasted_iota(jnp.int32, (16, 128), 1)
    first = lane < NLAT
    degree = lax.broadcasted_iota(jnp.int32, (16, NL), 1)
    none = jnp.zeros((16, 128), F32)
    for q in range(SLOTS // 4):
        g, half = divmod(q, 2)
        left = []
        for n in range(4):
            b = 4 * half + n
            mode = mode_ref[base + g * LANE_SLOTS + b]
            keep = mode.astype(F32) < limit
            own = first if n % 2 == 0 else ~first
            value = spread[16 * b : 16 * b + 16, g * 128 : (g + 1) * 128]
            value = jnp.where(keep & own, value, none)
            left.append(jnp.concatenate([value, none] if n < 2 else [none, value], axis=1))
        left = jnp.concatenate(left, axis=0).astype(BF16)
        result = dot(left, legendre_ref[q], ((1,), (0,)))
        for n in range(4):
            slot = 4 * q + n
            mode = mode_ref[base + slot]
            block = jnp.where(degree >= mode, result[16 * n : 16 * n + 16], 0.0)
            for r in range(2):
                for f in range(FIELDS):
                    at = (r * FIELDS + f) * PER_PEER
                    out_ref[slot, r, f] = block[at : at + PER_PEER].astype(BF16)


def params():
    return pltpu.CompilerParams(vmem_limit_bytes=VMEM)


def in_vmem():
    return pl.BlockSpec(memory_space=pltpu.VMEM)


def in_smem():
    return pl.BlockSpec(memory_space=pltpu.SMEM)


def per_device(grid_cot, weights, offsets, lat_points, slot_mode, legendre):
    sent = pl.pallas_call(
        deposit_kernel,
        name="deposit",
        out_shape=jax.ShapeDtypeStruct((SECTORS, LINES, WIDE), BF16),
        in_specs=[in_vmem()] * 4,
        out_specs=in_vmem(),
        scratch_shapes=[
            pltpu.VMEM((2 * REACH + 1, ROWS, 3, LEV, COLS), F32),
            pltpu.VMEM((FIELDS * TARGETS * LEV, WIDE), F32),
        ],
        compiler_params=params(),
        cost_estimate=pl.CostEstimate(flops=20_000_000, bytes_accessed=1_500_000, transcendentals=0),
    )(grid_cot, weights, offsets, jnp.asarray(level_order()))
    column_mode = slot_mode.reshape(M // LANE_SLOTS, LANE_SLOTS).T.reshape(1, M)
    table, turn = pl.pallas_call(
        table_kernel,
        name="table",
        out_shape=(
            jax.ShapeDtypeStruct((WIDE, 2 * M), BF16),
            jax.ShapeDtypeStruct((2, SECTORS, M), F32),
        ),
        in_specs=[in_vmem()],
        out_specs=(in_vmem(), in_vmem()),
        compiler_params=params(),
        cost_estimate=pl.CostEstimate(flops=20_000_000, bytes_accessed=4_000_000, transcendentals=0),
    )(column_mode)
    circles = lax.all_to_all(sent, "lon", split_axis=0, concat_axis=0, tiled=True)
    message = pl.pallas_call(
        fourier_kernel,
        name="fourier",
        out_shape=jax.ShapeDtypeStruct((BANDS, MSG, 128), BF16),
        in_specs=[in_smem()] + [in_vmem()] * 4,
        out_specs=in_vmem(),
        scratch_shapes=[
            pltpu.VMEM((TARGETS, 16, M), BF16),
            pltpu.VMEM((128, TARGETS * BANDS * GROUPS), BF16),
        ],
        compiler_params=params(),
        cost_estimate=pl.CostEstimate(flops=1_000_000_000, bytes_accessed=5_000_000, transcendentals=0),
    )(lat_points, circles, table, turn, jnp.asarray(message_order()))
    coefficients = lax.all_to_all(message, "lat", split_axis=0, concat_axis=0, tiled=True)
    band = lax.axis_index("lat").astype(jnp.int32).reshape(1)
    return pl.pallas_call(
        legendre_kernel,
        name="legendre",
        out_shape=jax.ShapeDtypeStruct((SLOTS, 2, FIELDS, PER_PEER, NL), BF16),
        in_specs=[in_smem(), in_smem()] + [in_vmem()] * 3,
        out_specs=in_vmem(),
        compiler_params=params(),
        cost_estimate=pl.CostEstimate(flops=500_000_000, bytes_accessed=8_000_000, transcendentals=0),
    )(
        slot_mode,
        band,
        coefficients,
        legendre.reshape(SLOTS // 4, 4 * NLAT, NL),
        jnp.asarray(latitude_order()),
    )


def solution(mesh):
    placed = (
        P(None, "lat", None, "lon"),
        P("lat", None, None, "lon"),
        P("lat", None, None, "lon"),
        P("lat"),
        P(),
        P("lat", None, None),
    )
    return jax.shard_map(
        per_device,
        mesh=mesh,
        in_specs=placed,
        out_specs=P("lat", None, None, "lon", None),
        check_vma=False,
    )
```

```python
import functools

import jax
import jax.numpy as jnp
import numpy as np
from jax import lax
from jax.experimental import pallas as pl
from jax.experimental.pallas import tpu as pltpu
from jax.sharding import PartitionSpec as P

FIELDS = 4
NLON = 5120
M = 1280
NL = 1280
REACH = 4
LEV = 16
ROWS = 2
TARGETS = ROWS + 2
SECTORS = 8
BANDS = 32
COLS = NLON // SECTORS
WIDE = 768
PER_PEER = LEV // SECTORS
LINES = TARGETS * FIELDS * PER_PEER
SLOTS = M // BANDS
LANE_SLOTS = 8
GROUPS = SLOTS // LANE_SLOTS
MSG = TARGETS * (GROUPS + 1)
NLAT = ROWS * BANDS

F32 = jnp.float32
BF16 = jnp.bfloat16


def dot(a, b, dims):
    return lax.dot_general(a, b, (dims, ((), ())), preferred_element_type=F32)


def spread_order():
    order = np.zeros((6 * ROWS * LEV, 6 * FIELDS * ROWS * LEV), np.float32)
    for c in range(6):
        for f in range(FIELDS):
            for n in range(ROWS * LEV):
                row = n * 4 + c if c < 4 else ROWS * LEV * 4 + n * 2 + c - 4
                order[row, (c * FIELDS + f) * ROWS * LEV + n] = 1
    return order.astype(BF16)


def level_order():
    order = np.zeros((SECTORS * LINES, 3, 2, FIELDS, ROWS, LEV), np.float32)
    for peer in range(SECTORS):
        for t in range(TARGETS):
            for f in range(FIELDS):
                for v in range(PER_PEER):
                    out = ((peer * TARGETS + t) * FIELDS + f) * PER_PEER + v
                    for i in range(ROWS):
                        if 0 <= t - i < 3:
                            order[out, t - i, :, f, i, peer * PER_PEER + v] = 1
    return order.reshape(SECTORS * LINES, -1).astype(BF16)


def message_order():
    order = np.zeros((BANDS * MSG, TARGETS * BANDS * GROUPS), np.float32)
    for k in range(BANDS):
        for t in range(TARGETS):
            for g in range(GROUPS):
                order[k * MSG + t * (GROUPS + 1) + g, (t * BANDS + k) * GROUPS + g] = 1
    return order.astype(BF16)


def latitude_order():
    order = np.zeros((BANDS * MSG, (GROUPS + 1) * 2 * NLAT), np.float32)
    for k in range(BANDS):
        for t in range(TARGETS):
            i = ROWS * k + t - 1
            if 0 <= i < NLAT:
                for g in range(GROUPS + 1):
                    for twice in range(2):
                        order[k * MSG + t * (GROUPS + 1) + g, (g * 2 + twice) * NLAT + i] = 1
    return order.astype(BF16)


LANES = FIELDS * ROWS * LEV


def deposit_kernel(
    grid_hbm, weight_hbm, offset_hbm, spread_hbm, order_hbm, out_ref,
    grid, weight, offset, spread, order, sems, stacked, wide, terms, parts,
):
    pairs = (
        (offset_hbm, offset), (weight_hbm, weight), (spread_hbm, spread), (grid_hbm, grid), (order_hbm, order),
    )
    copies = [pltpu.make_async_copy(src, dst, sems.at[n]) for n, (src, dst) in enumerate(pairs)]
    for copy in copies:
        copy.start()
    for n in range(7):
        fill = jnp.full((8, LANES), 99.0 if n == 0 else 0.0, F32)
        terms[n, 0:8] = fill
        terms[n, COLS + 8 : COLS + 16] = fill
    copies[0].wait()
    for i in range(ROWS):
        for v in range(LEV):
            at = ROWS * LEV * 4 + (i * LEV + v) * 2
            stacked[at : at + 2, :] = offset[i, v].astype(F32)
    copies[1].wait()
    for i in range(ROWS):
        for v in range(LEV):
            at = (i * LEV + v) * 4
            stacked[at : at + 4, :] = weight[i, v].astype(F32)
    copies[2].wait()
    wide[...] = dot(stacked[...].astype(BF16), spread[...], ((0,), (0,)))
    copies[3].wait()
    for j in range(COLS // 128):
        rows = slice(128 * j, 128 * j + 128)
        lines = slice(128 * j + 8, 128 * j + 136)
        g = grid[:, :, :, rows].reshape(LANES, 128).T
        w = [g * wide[rows, c * LANES : (c + 1) * LANES] for c in range(4)]
        south = wide[rows, 4 * LANES : 5 * LANES] < -0.5
        terms[0, lines] = wide[rows, 5 * LANES :]
        for q in range(2):
            terms[1 + q, lines] = jnp.where(south, w[q], 0.0)
            terms[3 + q, lines] = jnp.where(south, w[2 + q], w[q])
            terms[5 + q, lines] = jnp.where(south, 0.0, w[2 + q])

    def tile(start):
        total = [jnp.zeros((8, LANES), F32) for _ in range(3)]
        for n in range(2 * REACH + 1):
            shift = REACH - n
            east = terms[0, pl.ds(start + n, 8), :]
            here = east == float(shift)
            before = east == float(shift - 1)
            for r in range(3):
                first = terms[1 + 2 * r, pl.ds(start + n, 8), :]
                second = terms[2 + 2 * r, pl.ds(start + n, 8), :]
                total[r] = total[r] + jnp.where(here, first, jnp.where(before, second, 0.0))
        return total

    def step(n, carry):
        start = pl.multiple_of(n * 16, 16)
        top = tile(start)
        bottom = tile(start + 8)
        for r in range(3):
            whole = jnp.concatenate([top[r], bottom[r]], axis=0)
            high = whole.astype(BF16)
            low = (whole - high.astype(F32)).astype(BF16)
            parts[pl.ds(start, 16), 2 * r * LANES : (2 * r + 1) * LANES] = high
            parts[pl.ds(start, 16), (2 * r + 1) * LANES : (2 * r + 2) * LANES] = low
        return carry

    lax.fori_loop(0, COLS // 16, step, 0)
    edge = tile(COLS)
    parts[COLS:, :] = jnp.zeros((WIDE - COLS, 6 * LANES), BF16)
    for r in range(3):
        whole = jnp.concatenate([edge[r], jnp.zeros((8, LANES), F32)], axis=0)
        high = whole.astype(BF16)
        low = (whole - high.astype(F32)).astype(BF16)
        parts[COLS : COLS + 16, 2 * r * LANES : (2 * r + 1) * LANES] = high
        parts[COLS : COLS + 16, (2 * r + 1) * LANES : (2 * r + 2) * LANES] = low
    copies[4].wait()
    ordered = dot(order[...], parts[...], ((1,), (1,)))
    out_ref[...] = ordered.astype(BF16).reshape(out_ref.shape)


def sincos(count):
    turn = count - NLON * jnp.round(count * (1.0 / NLON))
    quarter = jnp.round(turn * (4.0 / NLON))
    x = (turn - (NLON // 4) * quarter) * np.float32(2.0 * np.pi / NLON)
    y = x * x
    s = x * (1.0 + y * (-1.0 / 6 + y * (1.0 / 120 + y * (-1.0 / 5040 + y * (1.0 / 362880)))))
    c = 1.0 + y * (-1.0 / 2 + y * (1.0 / 24 + y * (-1.0 / 720 + y * (1.0 / 40320))))
    odd = jnp.abs(quarter) == 1.0
    cosine = jnp.where(odd, s, c)
    sine = jnp.where(odd, c, s)
    cosine = jnp.where((quarter == 1.0) | (jnp.abs(quarter) == 2.0), -cosine, cosine)
    sine = jnp.where((quarter == -1.0) | (jnp.abs(quarter) == 2.0), -sine, sine)
    return cosine, sine


STEP = 32
BLOCK = 256
BLOCKS = M // BLOCK
AUX = 24


def table_kernel(points_ref, mode_ref, table_hbm, aux_hbm, table, aux, sems):
    mode = mode_ref[...].astype(F32)

    def rows(count, scale, first):
        index = lax.broadcasted_iota(jnp.int32, (count, M), 0) * scale + first
        return sincos(index.astype(F32) * mode)

    coarse_c, coarse_s = rows(WIDE // STEP, STEP, 0)
    fine_c, fine_s = rows(STEP, 1, -REACH)
    factor = jnp.where(mode == 0.0, 1.0, 2.0)
    fine_c = fine_c * factor
    fine_s = fine_s * factor
    copies = []
    for n in range(BLOCKS):
        part = slice(n * BLOCK, (n + 1) * BLOCK)
        for a in range(WIDE // STEP):
            c = coarse_c[a : a + 1, part]
            s = coarse_s[a : a + 1, part]
            lines = slice(a * STEP, (a + 1) * STEP)
            table[n, lines, :BLOCK] = (c * fine_c[:, part] - s * fine_s[:, part]).astype(BF16)
            table[n, lines, BLOCK:] = (-s * fine_c[:, part] - c * fine_s[:, part]).astype(BF16)
        copies.append(pltpu.make_async_copy(table.at[n], table_hbm.at[n], sems.at[n]))
        copies[-1].start()
    turn_c, turn_s = rows(SECTORS, COLS, 0)
    aux[0:SECTORS, :] = turn_c
    aux[SECTORS : 2 * SECTORS, :] = turn_s
    row = lax.broadcasted_iota(jnp.int32, (AUX - 2 * SECTORS, M), 0)
    lane = lax.broadcasted_iota(jnp.int32, (AUX - 2 * SECTORS, M), 1)
    extra = jnp.zeros((AUX - 2 * SECTORS, M), F32)
    for i in range(ROWS):
        count = (points_ref[i] + 1) // 2
        high = count // 16
        value = jnp.where(lane == 0, high, jnp.where(lane == 1, count - 16 * high, 0))
        extra = extra + jnp.where(row == i, value, 0).astype(F32)
    aux[2 * SECTORS :, :] = extra
    copies.append(pltpu.make_async_copy(aux, aux_hbm, sems.at[BLOCKS]))
    copies[-1].start()
    for copy in copies:
        copy.wait()


def fourier_kernel(grid_ref, table_hbm, aux_hbm, order_hbm, out_ref, table, aux, order, sems, spectra, lanes):
    copies = [pltpu.make_async_copy(aux_hbm, aux, sems.at[BLOCKS])]
    copies += [pltpu.make_async_copy(table_hbm.at[n], table.at[n], sems.at[n]) for n in range(BLOCKS)]
    copies.append(pltpu.make_async_copy(order_hbm, order, sems.at[BLOCKS + 1]))
    for copy in copies:
        copy.start()
    copies[0].wait()
    data = grid_ref[...].reshape(SECTORS * LINES, WIDE)
    for n in range(BLOCKS):
        part = slice(n * BLOCK, (n + 1) * BLOCK)
        copies[1 + n].wait()
        real = dot(data, table[n, :, :BLOCK], ((1,), (0,)))
        imag = dot(data, table[n, :, BLOCK:], ((1,), (0,)))
        sum_r = jnp.zeros((LINES, BLOCK), F32)
        sum_i = jnp.zeros((LINES, BLOCK), F32)
        for j in range(SECTORS):
            c = aux[j : j + 1, part]
            s = aux[SECTORS + j : SECTORS + j + 1, part]
            re = real[j * LINES : (j + 1) * LINES]
            im = imag[j * LINES : (j + 1) * LINES]
            sum_r = sum_r + c * re + s * im
            sum_i = sum_i + c * im - s * re
        for t in range(TARGETS):
            rows = slice(8 * t, 8 * t + 8)
            spectra[t, :, part] = jnp.concatenate([sum_r[rows], sum_i[rows]], axis=0).astype(BF16)
    run = BANDS * GROUPS
    for t in range(TARGETS):
        for b in range(LANE_SLOTS):
            lanes[16 * b : 16 * b + 16, t * run : (t + 1) * run] = spectra[t, :, b * run : (b + 1) * run]
    copies[-1].wait()
    message = dot(order[...], lanes[...], ((1,), (1,)))
    row = lax.broadcasted_iota(jnp.int32, (MSG, 128), 0)
    extra = jnp.zeros((MSG, 128), F32)
    for i in range(ROWS):
        limit = aux[2 * SECTORS + i : 2 * SECTORS + i + 1, 0:128]
        extra = jnp.where(row == (i + 1) * (GROUPS + 1) + GROUPS, limit, extra)
    for k in range(BANDS):
        out_ref[k] = (message[k * MSG : (k + 1) * MSG] + extra).astype(BF16)


def legendre_kernel(mode_ref, msg_ref, legendre_hbm, order_hbm, out_hbm, legendre, order, out, sems):
    quads = SLOTS // 4
    copies = [pltpu.make_async_copy(order_hbm, order, sems.at[quads])]
    copies += [pltpu.make_async_copy(legendre_hbm.at[q], legendre.at[q], sems.at[q]) for q in range(quads)]
    for copy in copies:
        copy.start()
    base = lax.axis_index("lat") * SLOTS
    received = msg_ref[...].reshape(BANDS * MSG, 128)
    copies[0].wait()
    spread = dot(received, order[...], ((0,), (0,)))
    lp = spread[:, GROUPS * 128 :]
    limit = 16.0 * lp[0:1] + lp[1:2]
    lane = lax.broadcasted_iota(jnp.int32, (16, 128), 1)
    first = lane < NLAT
    degree = lax.broadcasted_iota(jnp.int32, (16, NL), 1)
    none = jnp.zeros((16, 128), F32)
    sent = []
    for q in range(quads):
        g, half = divmod(q, 2)
        left = []
        for n in range(4):
            b = 4 * half + n
            mode = mode_ref[base + g * LANE_SLOTS + b]
            keep = mode.astype(F32) < limit
            own = first if n % 2 == 0 else ~first
            value = spread[16 * b : 16 * b + 16, g * 128 : (g + 1) * 128]
            value = jnp.where(keep & own, value, none)
            left.append(jnp.concatenate([value, none] if n < 2 else [none, value], axis=1))
        left = jnp.concatenate(left, axis=0).astype(BF16)
        copies[1 + q].wait()
        result = dot(left, legendre[q], ((1,), (0,)))
        for n in range(4):
            slot = 4 * q + n
            mode = mode_ref[base + slot]
            block = jnp.where(degree >= mode, result[16 * n : 16 * n + 16], 0.0)
            for r in range(2):
                for f in range(FIELDS):
                    at = (r * FIELDS + f) * PER_PEER
                    out[slot, r, f] = block[at : at + PER_PEER].astype(BF16)
        here = pl.ds(4 * q, 4)
        sent.append(pltpu.make_async_copy(out.at[here], out_hbm.at[here], sems.at[quads + 1 + q]))
        sent[-1].start()
    for copy in sent:
        copy.wait()


def params(mib):
    return pltpu.CompilerParams(vmem_limit_bytes=mib * 1024 * 1024)


def in_vmem():
    return pl.BlockSpec(memory_space=pltpu.VMEM)


def in_hbm():
    return pl.BlockSpec(memory_space=pltpu.HBM)


def in_smem():
    return pl.BlockSpec(memory_space=pltpu.SMEM)


def per_device(grid_cot, weights, offsets, lat_points, slot_mode, legendre):
    sent = pl.pallas_call(
        deposit_kernel,
        name="deposit",
        out_shape=jax.ShapeDtypeStruct((SECTORS, LINES, WIDE), BF16),
        in_specs=[in_hbm()] * 5,
        out_specs=in_vmem(),
        scratch_shapes=[
            pltpu.VMEM(grid_cot.shape, F32),
            pltpu.VMEM(weights.shape, BF16),
            pltpu.VMEM(offsets.shape, jnp.int32),
            pltpu.VMEM((6 * ROWS * LEV, 6 * LANES), BF16),
            pltpu.VMEM((SECTORS * LINES, 6 * LANES), BF16),
            pltpu.SemaphoreType.DMA((5,)),
            pltpu.VMEM((6 * ROWS * LEV, COLS), F32),
            pltpu.VMEM((COLS, 6 * LANES), F32),
            pltpu.VMEM((7, COLS + 16, LANES), F32),
            pltpu.VMEM((WIDE, 6 * LANES), BF16),
        ],
        compiler_params=params(14),
        cost_estimate=pl.CostEstimate(flops=20_000_000, bytes_accessed=1_500_000, transcendentals=0),
    )(grid_cot, weights, offsets, jnp.asarray(spread_order()), jnp.asarray(level_order()))
    column_mode = slot_mode.reshape(M // LANE_SLOTS, LANE_SLOTS).T.reshape(1, M)
    table, aux = pl.pallas_call(
        table_kernel,
        name="table",
        out_shape=(
            jax.ShapeDtypeStruct((BLOCKS, WIDE, 2 * BLOCK), BF16),
            jax.ShapeDtypeStruct((AUX, M), F32),
        ),
        in_specs=[in_smem(), in_vmem()],
        out_specs=(in_hbm(), in_hbm()),
        scratch_shapes=[
            pltpu.VMEM((BLOCKS, WIDE, 2 * BLOCK), BF16),
            pltpu.VMEM((AUX, M), F32),
            pltpu.SemaphoreType.DMA((BLOCKS + 1,)),
        ],
        compiler_params=params(12),
        cost_estimate=pl.CostEstimate(flops=20_000_000, bytes_accessed=4_000_000, transcendentals=0),
    )(lat_points, column_mode)
    circles = lax.all_to_all(sent, "lon", split_axis=0, concat_axis=0, tiled=True)
    message = pl.pallas_call(
        fourier_kernel,
        name="fourier",
        out_shape=jax.ShapeDtypeStruct((BANDS, MSG, 128), BF16),
        in_specs=[in_vmem()] + [in_hbm()] * 3,
        out_specs=in_vmem(),
        scratch_shapes=[
            pltpu.VMEM((BLOCKS, WIDE, 2 * BLOCK), BF16),
            pltpu.VMEM((AUX, M), F32),
            pltpu.VMEM((BANDS * MSG, TARGETS * BANDS * GROUPS), BF16),
            pltpu.SemaphoreType.DMA((BLOCKS + 2,)),
            pltpu.VMEM((TARGETS, 16, M), BF16),
            pltpu.VMEM((128, TARGETS * BANDS * GROUPS), BF16),
        ],
        compiler_params=params(14),
        cost_estimate=pl.CostEstimate(flops=1_000_000_000, bytes_accessed=5_000_000, transcendentals=0),
    )(circles, table, aux, jnp.asarray(message_order()))
    coefficients = lax.all_to_all(message, "lat", split_axis=0, concat_axis=0, tiled=True)
    shape = (SLOTS, 2, FIELDS, PER_PEER, NL)
    quads = SLOTS // 4
    return pl.pallas_call(
        legendre_kernel,
        name="legendre",
        out_shape=jax.ShapeDtypeStruct(shape, BF16),
        in_specs=[in_smem(), in_vmem()] + [in_hbm()] * 2,
        out_specs=in_hbm(),
        scratch_shapes=[
            pltpu.VMEM((quads, 4 * NLAT, NL), BF16),
            pltpu.VMEM((BANDS * MSG, (GROUPS + 1) * 2 * NLAT), BF16),
            pltpu.VMEM(shape, BF16),
            pltpu.SemaphoreType.DMA((2 * quads + 1,)),
        ],
        compiler_params=params(20),
        cost_estimate=pl.CostEstimate(flops=500_000_000, bytes_accessed=8_000_000, transcendentals=0),
    )(slot_mode, coefficients, legendre.reshape(quads, 4 * NLAT, NL), jnp.asarray(latitude_order()))


def solution(mesh):
    placed = (
        P(None, "lat", None, "lon"),
        P("lat", None, None, "lon"),
        P("lat", None, None, "lon"),
        P("lat"),
        P(),
        P("lat", None, None),
    )
    return jax.shard_map(
        per_device,
        mesh=mesh,
        in_specs=placed,
        out_specs=P("lat", None, None, "lon", None),
        check_vma=False,
    )
```

```python
import functools

import jax
import jax.numpy as jnp
import numpy as np
from jax import lax
from jax.experimental import pallas as pl
from jax.experimental.pallas import tpu as pltpu
from jax.sharding import PartitionSpec as P

FIELDS = 4
NLON = 5120
M = 1280
NL = 1280
REACH = 4
LEV = 16
ROWS = 2
TARGETS = ROWS + 2
SECTORS = 8
BANDS = 32
COLS = NLON // SECTORS
WIDE = 768
PER_PEER = LEV // SECTORS
LINES = TARGETS * FIELDS * PER_PEER
SLOTS = M // BANDS
LANE_SLOTS = 8
GROUPS = SLOTS // LANE_SLOTS
MSG = TARGETS * (GROUPS + 1)
NLAT = ROWS * BANDS

F32 = jnp.float32
BF16 = jnp.bfloat16


def dot(a, b, dims):
    return lax.dot_general(a, b, (dims, ((), ())), preferred_element_type=F32)


def spread_order():
    order = np.zeros((6 * ROWS * LEV, 6 * FIELDS * ROWS * LEV), np.float32)
    for c in range(6):
        for f in range(FIELDS):
            for n in range(ROWS * LEV):
                row = n * 4 + c if c < 4 else ROWS * LEV * 4 + n * 2 + c - 4
                order[row, (c * FIELDS + f) * ROWS * LEV + n] = 1
    return order.astype(BF16)


def level_order():
    order = np.zeros((SECTORS * LINES, 3, 2, FIELDS, ROWS, LEV), np.float32)
    for peer in range(SECTORS):
        for t in range(TARGETS):
            for f in range(FIELDS):
                for v in range(PER_PEER):
                    out = ((peer * TARGETS + t) * FIELDS + f) * PER_PEER + v
                    for i in range(ROWS):
                        if 0 <= t - i < 3:
                            order[out, t - i, :, f, i, peer * PER_PEER + v] = 1
    return order.reshape(SECTORS * LINES, -1).astype(BF16)


def message_order():
    order = np.zeros((BANDS * MSG, TARGETS * BANDS * GROUPS), np.float32)
    for k in range(BANDS):
        for t in range(TARGETS):
            for g in range(GROUPS):
                order[k * MSG + t * (GROUPS + 1) + g, (t * BANDS + k) * GROUPS + g] = 1
    return order.astype(BF16)


def latitude_order():
    order = np.zeros((BANDS * MSG, (GROUPS + 1) * 2 * NLAT), np.float32)
    for k in range(BANDS):
        for t in range(TARGETS):
            i = ROWS * k + t - 1
            if 0 <= i < NLAT:
                for g in range(GROUPS + 1):
                    for twice in range(2):
                        order[k * MSG + t * (GROUPS + 1) + g, (g * 2 + twice) * NLAT + i] = 1
    return order.astype(BF16)


LANES = FIELDS * ROWS * LEV


def deposit_kernel(
    grid_hbm, weight_hbm, offset_hbm, spread_hbm, order_hbm, out_ref,
    grid, weight, offset, spread, order, sems, stacked, wide, terms, parts,
):
    pairs = (
        (offset_hbm, offset), (weight_hbm, weight), (spread_hbm, spread), (grid_hbm, grid), (order_hbm, order),
    )
    copies = [pltpu.make_async_copy(src, dst, sems.at[n]) for n, (src, dst) in enumerate(pairs)]
    for copy in copies:
        copy.start()
    for n in range(7):
        fill = jnp.full((8, LANES), 99.0 if n == 0 else 0.0, F32)
        terms[n, 0:8] = fill
        terms[n, COLS + 8 : COLS + 16] = fill
    copies[0].wait()
    for i in range(ROWS):
        for v in range(LEV):
            at = ROWS * LEV * 4 + (i * LEV + v) * 2
            stacked[at : at + 2, :] = offset[i, v].astype(F32)
    copies[1].wait()
    for i in range(ROWS):
        for v in range(LEV):
            at = (i * LEV + v) * 4
            stacked[at : at + 4, :] = weight[i, v].astype(F32)
    copies[2].wait()
    wide[...] = dot(stacked[...].astype(BF16), spread[...], ((0,), (0,)))
    copies[3].wait()
    for j in range(COLS // 128):
        rows = slice(128 * j, 128 * j + 128)
        lines = slice(128 * j + 8, 128 * j + 136)
        g = grid[:, :, :, rows].reshape(LANES, 128).T
        w = [g * wide[rows, c * LANES : (c + 1) * LANES] for c in range(4)]
        south = wide[rows, 4 * LANES : 5 * LANES] < -0.5
        terms[0, lines] = wide[rows, 5 * LANES :]
        for q in range(2):
            terms[1 + q, lines] = jnp.where(south, w[q], 0.0)
            terms[3 + q, lines] = jnp.where(south, w[2 + q], w[q])
            terms[5 + q, lines] = jnp.where(south, 0.0, w[2 + q])

    def tile(start):
        total = [jnp.zeros((8, LANES), F32) for _ in range(3)]
        for n in range(2 * REACH + 1):
            shift = REACH - n
            east = terms[0, pl.ds(start + n, 8), :]
            here = east == float(shift)
            before = east == float(shift - 1)
            for r in range(3):
                first = terms[1 + 2 * r, pl.ds(start + n, 8), :]
                second = terms[2 + 2 * r, pl.ds(start + n, 8), :]
                total[r] = total[r] + jnp.where(here, first, jnp.where(before, second, 0.0))
        return total

    def step(n, carry):
        start = pl.multiple_of(n * 16, 16)
        top = tile(start)
        bottom = tile(start + 8)
        for r in range(3):
            whole = jnp.concatenate([top[r], bottom[r]], axis=0)
            high = whole.astype(BF16)
            low = (whole - high.astype(F32)).astype(BF16)
            parts[pl.ds(start, 16), 2 * r * LANES : (2 * r + 1) * LANES] = high
            parts[pl.ds(start, 16), (2 * r + 1) * LANES : (2 * r + 2) * LANES] = low
        return carry

    lax.fori_loop(0, COLS // 16, step, 0)
    edge = tile(COLS)
    parts[COLS:, :] = jnp.zeros((WIDE - COLS, 6 * LANES), BF16)
    for r in range(3):
        whole = jnp.concatenate([edge[r], jnp.zeros((8, LANES), F32)], axis=0)
        high = whole.astype(BF16)
        low = (whole - high.astype(F32)).astype(BF16)
        parts[COLS : COLS + 16, 2 * r * LANES : (2 * r + 1) * LANES] = high
        parts[COLS : COLS + 16, (2 * r + 1) * LANES : (2 * r + 2) * LANES] = low
    copies[4].wait()
    ordered = dot(order[...], parts[...], ((1,), (1,)))
    out_ref[...] = ordered.astype(BF16).reshape(out_ref.shape)


def sincos(count):
    turn = count - NLON * jnp.round(count * (1.0 / NLON))
    quarter = jnp.round(turn * (4.0 / NLON))
    x = (turn - (NLON // 4) * quarter) * np.float32(2.0 * np.pi / NLON)
    y = x * x
    s = x * (1.0 + y * (-1.0 / 6 + y * (1.0 / 120 + y * (-1.0 / 5040 + y * (1.0 / 362880)))))
    c = 1.0 + y * (-1.0 / 2 + y * (1.0 / 24 + y * (-1.0 / 720 + y * (1.0 / 40320))))
    odd = jnp.abs(quarter) == 1.0
    cosine = jnp.where(odd, s, c)
    sine = jnp.where(odd, c, s)
    cosine = jnp.where((quarter == 1.0) | (jnp.abs(quarter) == 2.0), -cosine, cosine)
    sine = jnp.where((quarter == -1.0) | (jnp.abs(quarter) == 2.0), -sine, sine)
    return cosine, sine


STEP = 32
BLOCK = 256
BLOCKS = M // BLOCK
AUX = 24


def table_kernel(points_ref, mode_ref, table_hbm, aux_hbm, table, aux, sems):
    mode = mode_ref[...].astype(F32)

    def rows(count, scale, first):
        index = lax.broadcasted_iota(jnp.int32, (count, M), 0) * scale + first
        return sincos(index.astype(F32) * mode)

    coarse_c, coarse_s = rows(WIDE // STEP, STEP, 0)
    fine_c, fine_s = rows(STEP, 1, -REACH)
    factor = jnp.where(mode == 0.0, 1.0, 2.0)
    fine_c = fine_c * factor
    fine_s = fine_s * factor
    copies = []
    for n in range(BLOCKS):
        part = slice(n * BLOCK, (n + 1) * BLOCK)
        for a in range(WIDE // STEP):
            c = coarse_c[a : a + 1, part]
            s = coarse_s[a : a + 1, part]
            lines = slice(a * STEP, (a + 1) * STEP)
            table[n, lines, :BLOCK] = (c * fine_c[:, part] - s * fine_s[:, part]).astype(BF16)
            table[n, lines, BLOCK:] = (-s * fine_c[:, part] - c * fine_s[:, part]).astype(BF16)
        copies.append(pltpu.make_async_copy(table.at[n], table_hbm.at[n], sems.at[n]))
        copies[-1].start()
    turn_c, turn_s = rows(SECTORS, COLS, 0)
    aux[0:SECTORS, :] = turn_c
    aux[SECTORS : 2 * SECTORS, :] = turn_s
    row = lax.broadcasted_iota(jnp.int32, (AUX - 2 * SECTORS, M), 0)
    lane = lax.broadcasted_iota(jnp.int32, (AUX - 2 * SECTORS, M), 1)
    extra = jnp.zeros((AUX - 2 * SECTORS, M), F32)
    for i in range(ROWS):
        count = (points_ref[i] + 1) // 2
        high = count // 16
        value = jnp.where(lane == 0, high, jnp.where(lane == 1, count - 16 * high, 0))
        extra = extra + jnp.where(row == i, value, 0).astype(F32)
    aux[2 * SECTORS :, :] = extra
    copies.append(pltpu.make_async_copy(aux, aux_hbm, sems.at[BLOCKS]))
    copies[-1].start()
    for copy in copies:
        copy.wait()


def fourier_kernel(grid_ref, table_hbm, aux_hbm, order_hbm, out_ref, table, aux, order, sems, spectra, lanes):
    copies = [pltpu.make_async_copy(aux_hbm, aux, sems.at[BLOCKS])]
    copies += [pltpu.make_async_copy(table_hbm.at[n], table.at[n], sems.at[n]) for n in range(BLOCKS)]
    copies.append(pltpu.make_async_copy(order_hbm, order, sems.at[BLOCKS + 1]))
    for copy in copies:
        copy.start()
    copies[0].wait()
    data = grid_ref[...].reshape(SECTORS * LINES, WIDE)
    for n in range(BLOCKS):
        part = slice(n * BLOCK, (n + 1) * BLOCK)
        copies[1 + n].wait()
        real = dot(data, table[n, :, :BLOCK], ((1,), (0,)))
        imag = dot(data, table[n, :, BLOCK:], ((1,), (0,)))
        sum_r = jnp.zeros((LINES, BLOCK), F32)
        sum_i = jnp.zeros((LINES, BLOCK), F32)
        for j in range(SECTORS):
            c = aux[j : j + 1, part]
            s = aux[SECTORS + j : SECTORS + j + 1, part]
            re = real[j * LINES : (j + 1) * LINES]
            im = imag[j * LINES : (j + 1) * LINES]
            sum_r = sum_r + c * re + s * im
            sum_i = sum_i + c * im - s * re
        for t in range(TARGETS):
            rows = slice(8 * t, 8 * t + 8)
            spectra[t, :, part] = jnp.concatenate([sum_r[rows], sum_i[rows]], axis=0).astype(BF16)
    run = BANDS * GROUPS
    for t in range(TARGETS):
        for b in range(LANE_SLOTS):
            lanes[16 * b : 16 * b + 16, t * run : (t + 1) * run] = spectra[t, :, b * run : (b + 1) * run]
    copies[-1].wait()
    message = dot(order[...], lanes[...], ((1,), (1,)))
    row = lax.broadcasted_iota(jnp.int32, (MSG, 128), 0)
    extra = jnp.zeros((MSG, 128), F32)
    for i in range(ROWS):
        limit = aux[2 * SECTORS + i : 2 * SECTORS + i + 1, 0:128]
        extra = jnp.where(row == (i + 1) * (GROUPS + 1) + GROUPS, limit, extra)
    for k in range(BANDS):
        out_ref[k] = (message[k * MSG : (k + 1) * MSG] + extra).astype(BF16)


def legendre_kernel(mode_ref, msg_ref, legendre_hbm, order_hbm, out_hbm, legendre, order, out, sems):
    quads = SLOTS // 4
    copies = [pltpu.make_async_copy(order_hbm, order, sems.at[quads])]
    copies += [pltpu.make_async_copy(legendre_hbm.at[q], legendre.at[q], sems.at[q]) for q in range(quads)]
    for copy in copies:
        copy.start()
    base = lax.axis_index("lat") * SLOTS
    received = msg_ref[...].reshape(BANDS * MSG, 128)
    copies[0].wait()
    spread = dot(received, order[...], ((0,), (0,)))
    lp = spread[:, GROUPS * 128 :]
    limit = 16.0 * lp[0:1] + lp[1:2]
    lane = lax.broadcasted_iota(jnp.int32, (16, 128), 1)
    first = lane < NLAT
    degree = lax.broadcasted_iota(jnp.int32, (16, NL), 1)
    none = jnp.zeros((16, 128), F32)
    sent = []
    for q in range(quads):
        g, half = divmod(q, 2)
        left = []
        for n in range(4):
            b = 4 * half + n
            mode = mode_ref[base + g * LANE_SLOTS + b]
            keep = mode.astype(F32) < limit
            own = first if n % 2 == 0 else ~first
            value = spread[16 * b : 16 * b + 16, g * 128 : (g + 1) * 128]
            value = jnp.where(keep & own, value, none)
            left.append(jnp.concatenate([value, none] if n < 2 else [none, value], axis=1))
        left = jnp.concatenate(left, axis=0).astype(BF16)
        copies[1 + q].wait()
        result = dot(left, legendre[q], ((1,), (0,)))
        for n in range(4):
            slot = 4 * q + n
            mode = mode_ref[base + slot]
            block = jnp.where(degree >= mode, result[16 * n : 16 * n + 16], 0.0)
            for r in range(2):
                for f in range(FIELDS):
                    at = (r * FIELDS + f) * PER_PEER
                    out[slot, r, f] = block[at : at + PER_PEER].astype(BF16)
        here = pl.ds(4 * q, 4)
        sent.append(pltpu.make_async_copy(out.at[here], out_hbm.at[here], sems.at[quads + 1 + q]))
        sent[-1].start()
    for copy in sent:
        copy.wait()


def params(mib):
    return pltpu.CompilerParams(vmem_limit_bytes=mib * 1024 * 1024)


def in_vmem():
    return pl.BlockSpec(memory_space=pltpu.VMEM)


def hbm(*arrays):
    return [pltpu.with_memory_space_constraint(x, pltpu.HBM) for x in arrays]


def in_hbm():
    return pl.BlockSpec(memory_space=pltpu.HBM)


def in_smem():
    return pl.BlockSpec(memory_space=pltpu.SMEM)


def per_device(grid_cot, weights, offsets, lat_points, slot_mode, legendre):
    sent = pl.pallas_call(
        deposit_kernel,
        name="deposit",
        out_shape=jax.ShapeDtypeStruct((SECTORS, LINES, WIDE), BF16),
        in_specs=[in_hbm()] * 5,
        out_specs=in_vmem(),
        scratch_shapes=[
            pltpu.VMEM(grid_cot.shape, F32),
            pltpu.VMEM(weights.shape, BF16),
            pltpu.VMEM(offsets.shape, jnp.int32),
            pltpu.VMEM((6 * ROWS * LEV, 6 * LANES), BF16),
            pltpu.VMEM((SECTORS * LINES, 6 * LANES), BF16),
            pltpu.SemaphoreType.DMA((5,)),
            pltpu.VMEM((6 * ROWS * LEV, COLS), F32),
            pltpu.VMEM((COLS, 6 * LANES), F32),
            pltpu.VMEM((7, COLS + 16, LANES), F32),
            pltpu.VMEM((WIDE, 6 * LANES), BF16),
        ],
        compiler_params=params(14),
        cost_estimate=pl.CostEstimate(flops=20_000_000, bytes_accessed=1_500_000, transcendentals=0),
    )(*hbm(grid_cot, weights, offsets, jnp.asarray(spread_order()), jnp.asarray(level_order())))
    column_mode = slot_mode.reshape(M // LANE_SLOTS, LANE_SLOTS).T.reshape(1, M)
    table, aux = pl.pallas_call(
        table_kernel,
        name="table",
        out_shape=(
            pltpu.HBM((BLOCKS, WIDE, 2 * BLOCK), BF16),
            pltpu.HBM((AUX, M), F32),
        ),
        in_specs=[in_smem(), in_vmem()],
        out_specs=(in_hbm(), in_hbm()),
        scratch_shapes=[
            pltpu.VMEM((BLOCKS, WIDE, 2 * BLOCK), BF16),
            pltpu.VMEM((AUX, M), F32),
            pltpu.SemaphoreType.DMA((BLOCKS + 1,)),
        ],
        compiler_params=params(12),
        cost_estimate=pl.CostEstimate(flops=20_000_000, bytes_accessed=4_000_000, transcendentals=0),
    )(lat_points, column_mode)
    circles = lax.all_to_all(sent, "lon", split_axis=0, concat_axis=0, tiled=True)
    message = pl.pallas_call(
        fourier_kernel,
        name="fourier",
        out_shape=jax.ShapeDtypeStruct((BANDS, MSG, 128), BF16),
        in_specs=[in_vmem()] + [in_hbm()] * 3,
        out_specs=in_vmem(),
        scratch_shapes=[
            pltpu.VMEM((BLOCKS, WIDE, 2 * BLOCK), BF16),
            pltpu.VMEM((AUX, M), F32),
            pltpu.VMEM((BANDS * MSG, TARGETS * BANDS * GROUPS), BF16),
            pltpu.SemaphoreType.DMA((BLOCKS + 2,)),
            pltpu.VMEM((TARGETS, 16, M), BF16),
            pltpu.VMEM((128, TARGETS * BANDS * GROUPS), BF16),
        ],
        compiler_params=params(14),
        cost_estimate=pl.CostEstimate(flops=1_000_000_000, bytes_accessed=5_000_000, transcendentals=0),
    )(circles, *hbm(table, aux, jnp.asarray(message_order())))
    coefficients = lax.all_to_all(message, "lat", split_axis=0, concat_axis=0, tiled=True)
    shape = (SLOTS, 2, FIELDS, PER_PEER, NL)
    quads = SLOTS // 4
    return pl.pallas_call(
        legendre_kernel,
        name="legendre",
        out_shape=jax.ShapeDtypeStruct(shape, BF16),
        in_specs=[in_smem(), in_vmem()] + [in_hbm()] * 2,
        out_specs=in_hbm(),
        scratch_shapes=[
            pltpu.VMEM((quads, 4 * NLAT, NL), BF16),
            pltpu.VMEM((BANDS * MSG, (GROUPS + 1) * 2 * NLAT), BF16),
            pltpu.VMEM(shape, BF16),
            pltpu.SemaphoreType.DMA((2 * quads + 1,)),
        ],
        compiler_params=params(20),
        cost_estimate=pl.CostEstimate(flops=500_000_000, bytes_accessed=8_000_000, transcendentals=0),
    )(slot_mode, coefficients, *hbm(legendre.reshape(quads, 4 * NLAT, NL), jnp.asarray(latitude_order())))


def solution(mesh):
    placed = (
        P(None, "lat", None, "lon"),
        P("lat", None, None, "lon"),
        P("lat", None, None, "lon"),
        P("lat"),
        P(),
        P("lat", None, None),
    )
    return jax.shard_map(
        per_device,
        mesh=mesh,
        in_specs=placed,
        out_specs=P("lat", None, None, "lon", None),
        check_vma=False,
    )
```

```python
import functools

import jax
import jax.numpy as jnp
import numpy as np
from jax import lax
from jax.experimental import pallas as pl
from jax.experimental.pallas import tpu as pltpu
from jax.sharding import PartitionSpec as P

FIELDS = 4
NLON = 5120
M = 1280
NL = 1280
REACH = 4
LEV = 16
ROWS = 2
TARGETS = ROWS + 2
SECTORS = 8
BANDS = 32
COLS = NLON // SECTORS
WIDE = 768
PER_PEER = LEV // SECTORS
LINES = TARGETS * FIELDS * PER_PEER
SLOTS = M // BANDS
LANE_SLOTS = 8
GROUPS = SLOTS // LANE_SLOTS
MSG = TARGETS * (GROUPS + 1)
NLAT = ROWS * BANDS

F32 = jnp.float32
BF16 = jnp.bfloat16


def dot(a, b, dims):
    return lax.dot_general(a, b, (dims, ((), ())), preferred_element_type=F32)


def one_hot(target, rows):
    row = lax.broadcasted_iota(jnp.int32, (rows, target.shape[1]), 0)
    return jnp.where(row == target, 1.0, 0.0).astype(BF16)


def spread_order():
    lane = lax.broadcasted_iota(jnp.int32, (1, 6 * LANES), 1)
    kind = lane // LANES
    place = (lane // (FIELDS * LEV)) % ROWS * LEV + lane % LEV
    return one_hot(jnp.where(kind < 4, place * 4 + kind, ROWS * LEV * 4 + place * 2 + kind - 4), 6 * ROWS * LEV)


def line_order():
    lane = lax.broadcasted_iota(jnp.int32, (1, 2 * LANES), 1)
    half = lane // (FIELDS * LEV) % 2
    target = jnp.where(lane < LANES, half * 3, half + 1)
    field = lane // LEV % FIELDS
    level = lane % LEV
    row = ((level // PER_PEER * TARGETS + target) * FIELDS + field) * PER_PEER + level % PER_PEER
    return one_hot(row, SECTORS * LINES)


UNROLL = 32
LANES = FIELDS * ROWS * LEV


def deposit_kernel(
    grid_hbm, weight_hbm, offset_hbm, out_ref, grid, weight, offset, sems, stacked, wide, terms, sums, parts
):
    pairs = ((offset_hbm, offset), (weight_hbm, weight), (grid_hbm, grid))
    copies = [pltpu.make_async_copy(src, dst, sems.at[n]) for n, (src, dst) in enumerate(pairs)]
    for copy in copies:
        copy.start()
    spread = spread_order()
    order = line_order()
    for n in range(7):
        fill = jnp.full((8, LANES), 99.0 if n == 0 else 0.0, F32)
        terms[n, 0:8] = fill
        terms[n, COLS + 8 : COLS + 16] = fill
    copies[0].wait()
    for i in range(ROWS):
        for v in range(LEV):
            at = ROWS * LEV * 4 + (i * LEV + v) * 2
            stacked[at : at + 2, :] = offset[i, v].astype(F32)
    copies[1].wait()
    for i in range(ROWS):
        for v in range(LEV):
            at = (i * LEV + v) * 4
            stacked[at : at + 4, :] = weight[i, v].astype(F32)
    wide[...] = dot(stacked[...].astype(BF16), spread, ((0,), (0,)))
    copies[2].wait()
    for j in range(COLS // 128):
        rows = slice(128 * j, 128 * j + 128)
        lines = slice(128 * j + 8, 128 * j + 136)
        g = jnp.concatenate([grid[:, i, :, rows].reshape(FIELDS * LEV, 128) for i in range(ROWS)], axis=0).T
        w = [g * wide[rows, c * LANES : (c + 1) * LANES] for c in range(4)]
        south = wide[rows, 4 * LANES : 5 * LANES] < -0.5
        terms[0, lines] = wide[rows, 5 * LANES :]
        for q in range(2):
            terms[1 + q, lines] = jnp.where(south, w[q], 0.0)
            terms[3 + q, lines] = jnp.where(south, w[2 + q], w[q])
            terms[5 + q, lines] = jnp.where(south, 0.0, w[2 + q])

    def tile(start):
        total = [jnp.zeros((8, LANES), F32) for _ in range(3)]
        for n in range(2 * REACH + 1):
            shift = REACH - n
            east = terms[0, pl.ds(start + n, 8), :]
            here = east == float(shift)
            before = east == float(shift - 1)
            for r in range(3):
                first = terms[1 + 2 * r, pl.ds(start + n, 8), :]
                second = terms[2 + 2 * r, pl.ds(start + n, 8), :]
                total[r] = total[r] + jnp.where(here, first, jnp.where(before, second, 0.0))
        return total

    def step(n, carry):
        start = pl.multiple_of(n * UNROLL, UNROLL)
        for m in range(0, UNROLL, 8):
            for r, total in enumerate(tile(start + m)):
                sums[r, pl.ds(start + m, 8), :] = total
        return carry

    lax.fori_loop(0, COLS // UNROLL, step, 0)
    for r, total in enumerate(tile(COLS)):
        sums[r, COLS : COLS + 8] = total
        sums[r, COLS + 8 :] = jnp.zeros((WIDE - COLS - 8, LANES), F32)
    north, same, south = sums[0], sums[1], sums[2]
    inner = lax.broadcasted_iota(jnp.int32, (1, LANES), 1) < FIELDS * LEV
    parts[:, :LANES] = jnp.where(inner, north, south).astype(BF16)
    parts[:, LANES:] = (same + pltpu.roll(jnp.where(inner, south, north), FIELDS * LEV, 1)).astype(BF16)
    ordered = dot(order, parts[...], ((1,), (1,)))
    out_ref[...] = ordered.astype(BF16).reshape(out_ref.shape)


def sincos(count):
    turn = count - NLON * jnp.round(count * (1.0 / NLON))
    quarter = jnp.round(turn * (4.0 / NLON))
    x = (turn - (NLON // 4) * quarter) * np.float32(2.0 * np.pi / NLON)
    y = x * x
    s = x * (1.0 + y * (-1.0 / 6 + y * (1.0 / 120 + y * (-1.0 / 5040 + y * (1.0 / 362880)))))
    c = 1.0 + y * (-1.0 / 2 + y * (1.0 / 24 + y * (-1.0 / 720 + y * (1.0 / 40320))))
    odd = jnp.abs(quarter) == 1.0
    cosine = jnp.where(odd, s, c)
    sine = jnp.where(odd, c, s)
    cosine = jnp.where((quarter == 1.0) | (jnp.abs(quarter) == 2.0), -cosine, cosine)
    sine = jnp.where((quarter == -1.0) | (jnp.abs(quarter) == 2.0), -sine, sine)
    return cosine, sine


STEP = 16
DEPTH = COLS + STEP
BLOCK = 256
BLOCKS = M // BLOCK
EARLY = 4
AUX = 24


def table_kernel(points_ref, mode_ref, *refs):
    early, (aux, table_hbm, late, sems) = refs[:EARLY], refs[EARLY:]
    table = [*early, *[late.at[n] for n in range(BLOCKS - EARLY)]]
    copies = []
    mode = mode_ref[...].astype(F32)

    def rows(count, scale, first):
        index = lax.broadcasted_iota(jnp.int32, (count, M), 0) * scale + first
        return sincos(index.astype(F32) * mode)

    coarse_c, coarse_s = rows(DEPTH // STEP, STEP, 0)
    fine_c, fine_s = rows(STEP, 1, -REACH)
    factor = jnp.where(mode == 0.0, 1.0, 2.0)
    fine_c = fine_c * factor
    fine_s = fine_s * factor
    for n in (*range(EARLY, BLOCKS), *range(EARLY)):
        part = slice(n * BLOCK, (n + 1) * BLOCK)
        for a in range(DEPTH // STEP):
            c = coarse_c[a : a + 1, part]
            s = coarse_s[a : a + 1, part]
            lines = slice(a * STEP, (a + 1) * STEP)
            table[n][lines, :BLOCK] = (c * fine_c[:, part] - s * fine_s[:, part]).astype(BF16)
            table[n][lines, BLOCK:] = (-s * fine_c[:, part] - c * fine_s[:, part]).astype(BF16)
        if n >= EARLY:
            copies.append(pltpu.make_async_copy(table[n], table_hbm.at[n - EARLY], sems.at[n - EARLY]))
            copies[-1].start()
    turn_c, turn_s = rows(SECTORS, COLS, 0)
    aux[0:SECTORS, :] = turn_c
    aux[SECTORS : 2 * SECTORS, :] = turn_s
    row = lax.broadcasted_iota(jnp.int32, (AUX - 2 * SECTORS, M), 0)
    lane = lax.broadcasted_iota(jnp.int32, (AUX - 2 * SECTORS, M), 1)
    extra = jnp.zeros((AUX - 2 * SECTORS, M), F32)
    for i in range(ROWS):
        count = (points_ref[i] + 1) // 2
        high = count // 16
        value = jnp.where(lane == 0, high, jnp.where(lane == 1, count - 16 * high, 0))
        extra = extra + jnp.where(row == i, value, 0).astype(F32)
    aux[2 * SECTORS :, :] = extra
    for copy in copies:
        copy.wait()


def fourier_kernel(grid_ref, *refs):
    early, (aux, table_hbm, out_ref, late, sem, spectra, lanes, rows) = refs[:EARLY], refs[EARLY:]
    table = [*early, *[late.at[n] for n in range(BLOCKS - EARLY)]]
    copy = pltpu.make_async_copy(table_hbm, late, sem)
    copy.start()
    data = grid_ref[...].reshape(SECTORS * LINES, WIDE)[:, :DEPTH]
    for n in range(BLOCKS):
        part = slice(n * BLOCK, (n + 1) * BLOCK)
        if n == EARLY:
            copy.wait()
        real = dot(data, table[n][:, :BLOCK], ((1,), (0,)))
        imag = dot(data, table[n][:, BLOCK:], ((1,), (0,)))
        sum_r = jnp.zeros((LINES, BLOCK), F32)
        sum_i = jnp.zeros((LINES, BLOCK), F32)
        for j in range(SECTORS):
            c = aux[j : j + 1, part]
            s = aux[SECTORS + j : SECTORS + j + 1, part]
            re = real[j * LINES : (j + 1) * LINES]
            im = imag[j * LINES : (j + 1) * LINES]
            sum_r = sum_r + c * re + s * im
            sum_i = sum_i + c * im - s * re
        for t in range(TARGETS):
            here = slice(8 * t, 8 * t + 8)
            spectra[t, :, part] = jnp.concatenate([sum_r[here], sum_i[here]], axis=0).astype(BF16)
    run = BANDS * GROUPS
    for t in range(TARGETS):
        for b in range(LANE_SLOTS):
            lanes[16 * b : 16 * b + 16, t * run : (t + 1) * run] = spectra[t, :, b * run : (b + 1) * run]
    turned = lanes[...].astype(F32).T
    for t in range(TARGETS):
        for g in range(GROUPS):
            at = (t * GROUPS + g) * BANDS
            rows[pl.ds(t * (GROUPS + 1) + g, BANDS, stride=MSG), :] = turned[at : at + BANDS]
        limit = jnp.zeros((BANDS, 128), F32)
        if 0 < t <= ROWS:
            limit = limit + aux[2 * SECTORS + t - 1 : 2 * SECTORS + t, 0:128]
        rows[pl.ds(t * (GROUPS + 1) + GROUPS, BANDS, stride=MSG), :] = limit
    out_ref[...] = rows[...].astype(BF16).reshape(out_ref.shape)


QUADS = SLOTS // 4
STAGED = 5
CUT = 8


def stage_kernel(legendre_hbm, *refs):
    *legendre, sems = refs
    copies = [pltpu.make_async_copy(legendre_hbm.at[q], legendre[q], sems.at[q]) for q in range(STAGED)]
    for copy in copies:
        copy.start()
    for copy in copies:
        copy.wait()


def legendre_kernel(mode_ref, msg_ref, *refs):
    early, (legendre_hbm, out_hbm, late, out, late_sems, sems, rows, mixed) = refs[:STAGED], refs[STAGED:]
    legendre = [*early, *[late.at[q] for q in range(QUADS - STAGED)]]
    copies = {
        first: pltpu.make_async_copy(
            legendre_hbm.at[pl.ds(first, last - first)], late.at[pl.ds(first - STAGED, last - first)], late_sems.at[n]
        )
        for n, (first, last) in enumerate(((STAGED, CUT), (CUT, QUADS)))
    }
    for copy in copies.values():
        copy.start()
    base = lax.axis_index("lat") * SLOTS
    rows[0:MSG] = jnp.zeros((MSG, 128), F32)
    rows[MSG : (BANDS + 1) * MSG] = msg_ref[...].reshape(BANDS * MSG, 128).astype(F32)
    rows[(BANDS + 1) * MSG :] = jnp.zeros((MSG, 128), F32)
    for g in range(GROUPS + 1):

        def part(t, neighbour):
            return rows[pl.ds((1 + neighbour) * MSG + t * (GROUPS + 1) + g, BANDS, stride=MSG), :]

        mixed[pl.ds(g * NLAT, BANDS, stride=2), :] = part(1, 0) + part(3, -1)
        mixed[pl.ds(g * NLAT + 1, BANDS, stride=2), :] = part(2, 0) + part(0, 1)
    spread = mixed[...].T
    lane = lax.broadcasted_iota(jnp.int32, (16, 128), 1)
    first = lane < NLAT
    plain = [spread[:, 128 * p : 128 * p + 128] for p in range((GROUPS + 1) // 2)]
    swapped = [pltpu.roll(p, NLAT, 1) for p in plain]
    limit = jnp.where(
        first[0:1],
        16.0 * swapped[-1][0:1] + swapped[-1][1:2],
        16.0 * plain[-1][0:1] + plain[-1][1:2],
    )
    degree = lax.broadcasted_iota(jnp.int32, (16, NL), 1)
    none = jnp.zeros((16, 128), F32)
    sent = []
    for q in range(QUADS):
        g, half = divmod(q, 2)
        left = []
        for n in range(4):
            b = 4 * half + n
            mode = mode_ref[base + g * LANE_SLOTS + b]
            keep = mode.astype(F32) < limit
            own = first if n % 2 == 0 else ~first
            value = (plain if g % 2 == n % 2 else swapped)[g // 2][16 * b : 16 * b + 16]
            value = jnp.where(keep & own, value, none)
            left.append(jnp.concatenate([value, none] if n < 2 else [none, value], axis=1))
        left = jnp.concatenate(left, axis=0).astype(BF16)
        if q in copies:
            copies[q].wait()
        result = dot(left, legendre[q][...], ((1,), (0,)))
        for n in range(4):
            slot = 4 * q + n
            mode = mode_ref[base + slot]
            block = jnp.where(degree >= mode, result[16 * n : 16 * n + 16], 0.0)
            for r in range(2):
                for f in range(FIELDS):
                    at = (r * FIELDS + f) * PER_PEER
                    out[slot, r, f] = block[at : at + PER_PEER].astype(BF16)
        here = pl.ds(4 * q, 4)
        sent.append(pltpu.make_async_copy(out.at[here], out_hbm.at[here], sems.at[q]))
        sent[-1].start()
    for copy in sent:
        copy.wait()


def params(mib):
    return pltpu.CompilerParams(vmem_limit_bytes=mib * 1024 * 1024)


def in_vmem():
    return pl.BlockSpec(memory_space=pltpu.VMEM)


def hbm(*arrays):
    return [pltpu.with_memory_space_constraint(x, pltpu.HBM) for x in arrays]


def vmem(*arrays):
    return [pltpu.with_memory_space_constraint(x, pltpu.VMEM) for x in arrays]


def in_hbm():
    return pl.BlockSpec(memory_space=pltpu.HBM)


def in_smem():
    return pl.BlockSpec(memory_space=pltpu.SMEM)


def per_device(grid_cot, weights, offsets, lat_points, slot_mode, legendre):
    sent = pl.pallas_call(
        deposit_kernel,
        name="deposit",
        out_shape=pltpu.VMEM((SECTORS, LINES, WIDE), BF16),
        in_specs=[in_hbm()] * 3,
        out_specs=in_vmem(),
        scratch_shapes=[
            pltpu.VMEM(grid_cot.shape, F32),
            pltpu.VMEM(weights.shape, BF16),
            pltpu.VMEM(offsets.shape, jnp.int32),
            pltpu.SemaphoreType.DMA((3,)),
            pltpu.VMEM((6 * ROWS * LEV, COLS), F32),
            pltpu.VMEM((COLS, 6 * LANES), F32),
            pltpu.VMEM((7, COLS + 16, LANES), F32),
            pltpu.VMEM((3, WIDE, LANES), F32),
            pltpu.VMEM((WIDE, 2 * LANES), BF16),
        ],
        compiler_params=params(14),
        cost_estimate=pl.CostEstimate(flops=20_000_000, bytes_accessed=1_500_000, transcendentals=0),
    )(*hbm(grid_cot, weights, offsets))
    column_mode = slot_mode.reshape(BANDS, GROUPS, LANE_SLOTS).transpose(2, 1, 0).reshape(1, M)
    *tables, table_rest = pl.pallas_call(
        table_kernel,
        name="table",
        out_shape=(
            *[pltpu.VMEM((DEPTH, 2 * BLOCK), BF16)] * EARLY,
            pltpu.VMEM((AUX, M), F32),
            pltpu.HBM((BLOCKS - EARLY, DEPTH, 2 * BLOCK), BF16),
        ),
        in_specs=[in_smem(), in_vmem()],
        out_specs=(*[in_vmem()] * (EARLY + 1), in_hbm()),
        scratch_shapes=[
            pltpu.VMEM((BLOCKS - EARLY, DEPTH, 2 * BLOCK), BF16),
            pltpu.SemaphoreType.DMA((BLOCKS - EARLY,)),
        ],
        compiler_params=params(12),
        cost_estimate=pl.CostEstimate(flops=20_000_000, bytes_accessed=4_000_000, transcendentals=0),
    )(lat_points, column_mode)
    circles = lax.all_to_all(sent, "lon", split_axis=0, concat_axis=0, tiled=True)
    message = pl.pallas_call(
        fourier_kernel,
        name="fourier",
        out_shape=pltpu.VMEM((BANDS, MSG, 128), BF16),
        in_specs=[in_vmem()] * (EARLY + 2) + [in_hbm()],
        out_specs=in_vmem(),
        scratch_shapes=[
            pltpu.VMEM((BLOCKS - EARLY, DEPTH, 2 * BLOCK), BF16),
            pltpu.SemaphoreType.DMA,
            pltpu.VMEM((TARGETS, 16, M), BF16),
            pltpu.VMEM((128, TARGETS * BANDS * GROUPS), BF16),
            pltpu.VMEM((BANDS * MSG, 128), F32),
        ],
        compiler_params=params(14),
        cost_estimate=pl.CostEstimate(flops=1_000_000_000, bytes_accessed=5_000_000, transcendentals=0),
    )(circles, *vmem(*tables), *hbm(table_rest))
    shape = (SLOTS, 2, FIELDS, PER_PEER, NL)
    message, legendre = lax.optimization_barrier((message, legendre.reshape(QUADS, 4 * NLAT, NL)))
    staged = pl.pallas_call(
        stage_kernel,
        name="stage",
        out_shape=(
            *[pltpu.VMEM((4 * NLAT, NL), BF16)] * STAGED,
        ),
        in_specs=[in_hbm()],
        out_specs=(in_vmem(),) * STAGED,
        scratch_shapes=[pltpu.SemaphoreType.DMA((STAGED,))],
        compiler_params=params(12),
        cost_estimate=pl.CostEstimate(flops=0, bytes_accessed=16_000_000, transcendentals=0),
    )(*hbm(legendre))
    coefficients = lax.all_to_all(message, "lat", split_axis=0, concat_axis=0, tiled=True)
    return pl.pallas_call(
        legendre_kernel,
        name="legendre",
        out_shape=jax.ShapeDtypeStruct(shape, BF16),
        in_specs=[in_smem()] + [in_vmem()] * (STAGED + 1) + [in_hbm()],
        out_specs=in_hbm(),
        scratch_shapes=[
            pltpu.VMEM((QUADS - STAGED, 4 * NLAT, NL), BF16),
            pltpu.VMEM(shape, BF16),
            pltpu.SemaphoreType.DMA((2,)),
            pltpu.SemaphoreType.DMA((QUADS,)),
            pltpu.VMEM(((BANDS + 2) * MSG, 128), F32),
            pltpu.VMEM(((GROUPS + 1) * NLAT, 128), F32),
        ],
        compiler_params=params(12),
        cost_estimate=pl.CostEstimate(flops=500_000_000, bytes_accessed=8_000_000, transcendentals=0),
    )(slot_mode, coefficients, *vmem(*staged), *hbm(legendre))


def solution(mesh):
    placed = (
        P(None, "lat", None, "lon"),
        P("lat", None, None, "lon"),
        P("lat", None, None, "lon"),
        P("lat"),
        P(),
        P("lat", None, None),
    )
    return jax.shard_map(
        per_device,
        mesh=mesh,
        in_specs=placed,
        out_specs=P("lat", None, None, "lon", None),
        check_vma=False,
    )
```

```python
import functools

import jax
import jax.numpy as jnp
import numpy as np
from jax import lax
from jax.experimental import pallas as pl
from jax.experimental.pallas import tpu as pltpu
from jax.sharding import PartitionSpec as P

FIELDS = 4
NLON = 5120
M = 1280
NL = 1280
REACH = 4
LEV = 16
ROWS = 2
TARGETS = ROWS + 2
SECTORS = 8
BANDS = 32
COLS = NLON // SECTORS
WIDE = 768
PER_PEER = LEV // SECTORS
LINES = TARGETS * FIELDS * PER_PEER
SLOTS = M // BANDS
LANE_SLOTS = 8
GROUPS = SLOTS // LANE_SLOTS
MSG = TARGETS * (GROUPS + 1)
NLAT = ROWS * BANDS

F32 = jnp.float32
BF16 = jnp.bfloat16


def dot(a, b, dims):
    return lax.dot_general(a, b, (dims, ((), ())), preferred_element_type=F32)


def one_hot(target, rows):
    row = lax.broadcasted_iota(jnp.int32, (rows, target.shape[1]), 0)
    return jnp.where(row == target, 1.0, 0.0).astype(BF16)


def spread_order():
    lane = lax.broadcasted_iota(jnp.int32, (1, 6 * LANES), 1)
    kind = lane // LANES
    place = (lane // (FIELDS * LEV)) % ROWS * LEV + lane % LEV
    return one_hot(jnp.where(kind < 4, place * 4 + kind, ROWS * LEV * 4 + place * 2 + kind - 4), 6 * ROWS * LEV)


def line_order():
    lane = lax.broadcasted_iota(jnp.int32, (1, 2 * LANES), 1)
    half = lane // (FIELDS * LEV) % 2
    target = jnp.where(lane < LANES, half * 3, half + 1)
    field = lane // LEV % FIELDS
    level = lane % LEV
    row = ((level // PER_PEER * TARGETS + target) * FIELDS + field) * PER_PEER + level % PER_PEER
    return one_hot(row, SECTORS * LINES)


UNROLL = 128
LANES = FIELDS * ROWS * LEV


def deposit_kernel(
    grid_hbm, weight_hbm, offset_hbm, out_ref, grid, weight, offset, sems, stacked, wide, terms, sums, parts
):
    pairs = ((offset_hbm, offset), (weight_hbm, weight), (grid_hbm, grid))
    copies = [pltpu.make_async_copy(src, dst, sems.at[n]) for n, (src, dst) in enumerate(pairs)]
    for copy in copies:
        copy.start()
    spread = spread_order()
    order = line_order()
    for n in range(7):
        fill = jnp.full((8, LANES), 99.0 if n == 0 else 0.0, F32)
        terms[n, 0:8] = fill
        terms[n, COLS + 8 : COLS + 16] = fill
    copies[0].wait()
    for i in range(ROWS):
        for v in range(LEV):
            at = ROWS * LEV * 4 + (i * LEV + v) * 2
            stacked[at : at + 2, :] = offset[i, v].astype(F32)
    copies[1].wait()
    for i in range(ROWS):
        for v in range(LEV):
            at = (i * LEV + v) * 4
            stacked[at : at + 4, :] = weight[i, v].astype(F32)
    wide[...] = dot(stacked[...].astype(BF16), spread, ((0,), (0,)))
    copies[2].wait()
    for j in range(COLS // 128):
        rows = slice(128 * j, 128 * j + 128)
        lines = slice(128 * j + 8, 128 * j + 136)
        g = jnp.concatenate([grid[:, i, :, rows].reshape(FIELDS * LEV, 128) for i in range(ROWS)], axis=0).T
        w = [g * wide[rows, c * LANES : (c + 1) * LANES] for c in range(4)]
        south = wide[rows, 4 * LANES : 5 * LANES] < -0.5
        terms[0, lines] = wide[rows, 5 * LANES :]
        for q in range(2):
            terms[1 + q, lines] = jnp.where(south, w[q], 0.0)
            terms[3 + q, lines] = jnp.where(south, w[2 + q], w[q])
            terms[5 + q, lines] = jnp.where(south, 0.0, w[2 + q])

    def tile(start):
        total = [jnp.zeros((8, LANES), F32) for _ in range(3)]
        for n in range(2 * REACH + 1):
            shift = REACH - n
            east = terms[0, pl.ds(start + n, 8), :]
            here = east == float(shift)
            before = east == float(shift - 1)
            for r in range(3):
                first = terms[1 + 2 * r, pl.ds(start + n, 8), :]
                second = terms[2 + 2 * r, pl.ds(start + n, 8), :]
                total[r] = total[r] + jnp.where(here, first, jnp.where(before, second, 0.0))
        return total

    def step(n, carry):
        start = pl.multiple_of(n * UNROLL, UNROLL)
        for m in range(0, UNROLL, 8):
            for r, total in enumerate(tile(start + m)):
                sums[r, pl.ds(start + m, 8), :] = total
        return carry

    lax.fori_loop(0, COLS // UNROLL, step, 0)
    for r, total in enumerate(tile(COLS)):
        sums[r, COLS : COLS + 8] = total
        sums[r, COLS + 8 :] = jnp.zeros((WIDE - COLS - 8, LANES), F32)
    north, same, south = sums[0], sums[1], sums[2]
    inner = lax.broadcasted_iota(jnp.int32, (1, LANES), 1) < FIELDS * LEV
    parts[:, :LANES] = jnp.where(inner, north, south).astype(BF16)
    parts[:, LANES:] = (same + pltpu.roll(jnp.where(inner, south, north), FIELDS * LEV, 1)).astype(BF16)
    ordered = dot(order, parts[...], ((1,), (1,)))
    out_ref[...] = ordered.astype(BF16).reshape(out_ref.shape)


def sincos(count):
    turn = count - NLON * jnp.round(count * (1.0 / NLON))
    quarter = jnp.round(turn * (4.0 / NLON))
    x = (turn - (NLON // 4) * quarter) * np.float32(2.0 * np.pi / NLON)
    y = x * x
    s = x * (1.0 + y * (-1.0 / 6 + y * (1.0 / 120 + y * (-1.0 / 5040 + y * (1.0 / 362880)))))
    c = 1.0 + y * (-1.0 / 2 + y * (1.0 / 24 + y * (-1.0 / 720 + y * (1.0 / 40320))))
    odd = jnp.abs(quarter) == 1.0
    cosine = jnp.where(odd, s, c)
    sine = jnp.where(odd, c, s)
    cosine = jnp.where((quarter == 1.0) | (jnp.abs(quarter) == 2.0), -cosine, cosine)
    sine = jnp.where((quarter == -1.0) | (jnp.abs(quarter) == 2.0), -sine, sine)
    return cosine, sine


STEP = 32
HALVES = 2
DEPTH = WIDE // HALVES
TURNS = HALVES * SECTORS
BLOCK = 256
BLOCKS = M // BLOCK
AUX = 2 * TURNS + 8


def table_kernel(points_ref, mode_ref, *refs):
    *table, aux = refs
    mode = mode_ref[...].astype(F32)

    def rows(count, position):
        place = position(lax.broadcasted_iota(jnp.int32, (count, M), 0))
        return sincos(place.astype(F32) * mode)

    coarse_c, coarse_s = rows(DEPTH // STEP, lambda n: n * STEP)
    fine_c, fine_s = rows(STEP, lambda n: n - REACH)
    factor = jnp.where(mode == 0.0, 1.0, 2.0)
    fine_c = fine_c * factor
    fine_s = fine_s * factor
    for n in range(BLOCKS):
        part = slice(n * BLOCK, (n + 1) * BLOCK)
        for a in range(DEPTH // STEP):
            c = coarse_c[a : a + 1, part]
            s = coarse_s[a : a + 1, part]
            lines = slice(a * STEP, (a + 1) * STEP)
            table[n][lines, :BLOCK] = (c * fine_c[:, part] - s * fine_s[:, part]).astype(BF16)
            table[n][lines, BLOCK:] = (-s * fine_c[:, part] - c * fine_s[:, part]).astype(BF16)
    turn_c, turn_s = rows(TURNS, lambda n: n % SECTORS * COLS + n // SECTORS * DEPTH)
    aux[0:TURNS, :] = turn_c
    aux[TURNS : 2 * TURNS, :] = turn_s
    row = lax.broadcasted_iota(jnp.int32, (AUX - 2 * TURNS, M), 0)
    lane = lax.broadcasted_iota(jnp.int32, (AUX - 2 * TURNS, M), 1)
    extra = jnp.zeros((AUX - 2 * TURNS, M), F32)
    for i in range(ROWS):
        count = (points_ref[i] + 1) // 2
        high = count // 16
        value = jnp.where(lane == 0, high, jnp.where(lane == 1, count - 16 * high, 0))
        extra = extra + jnp.where(row == i, value, 0).astype(F32)
    aux[2 * TURNS :, :] = extra


def fourier_kernel(grid_ref, *refs):
    *table, aux, out_ref, spectra, lanes, rows = refs
    data = [grid_ref[:, :, h * DEPTH : (h + 1) * DEPTH].reshape(SECTORS * LINES, DEPTH) for h in range(HALVES)]
    for n in range(BLOCKS):
        part = slice(n * BLOCK, (n + 1) * BLOCK)
        sum_r = jnp.zeros((LINES, BLOCK), F32)
        sum_i = jnp.zeros((LINES, BLOCK), F32)
        for h in range(HALVES):
            real = dot(data[h], table[n][:, :BLOCK], ((1,), (0,)))
            imag = dot(data[h], table[n][:, BLOCK:], ((1,), (0,)))
            for j in range(SECTORS):
                turn = h * SECTORS + j
                c = aux[turn : turn + 1, part]
                s = aux[TURNS + turn : TURNS + turn + 1, part]
                re = real[j * LINES : (j + 1) * LINES]
                im = imag[j * LINES : (j + 1) * LINES]
                sum_r = sum_r + c * re + s * im
                sum_i = sum_i + c * im - s * re
        for t in range(TARGETS):
            here = slice(8 * t, 8 * t + 8)
            spectra[t, :, part] = jnp.concatenate([sum_r[here], sum_i[here]], axis=0).astype(BF16)
    run = BANDS * GROUPS
    for t in range(TARGETS):
        for b in range(LANE_SLOTS):
            lanes[16 * b : 16 * b + 16, t * run : (t + 1) * run] = spectra[t, :, b * run : (b + 1) * run]
    turned = lanes[...].astype(F32).T
    for t in range(TARGETS):
        for g in range(GROUPS):
            at = (t * GROUPS + g) * BANDS
            rows[pl.ds(t * (GROUPS + 1) + g, BANDS, stride=MSG), :] = turned[at : at + BANDS]
        limit = jnp.zeros((BANDS, 128), F32)
        if 0 < t <= ROWS:
            limit = limit + aux[2 * TURNS + t - 1 : 2 * TURNS + t, 0:128]
        rows[pl.ds(t * (GROUPS + 1) + GROUPS, BANDS, stride=MSG), :] = limit
    out_ref[...] = rows[...].astype(BF16).reshape(out_ref.shape)


QUADS = SLOTS // 4
STAGED = 5
CUT = 8


def stage_kernel(legendre_hbm, *refs):
    *legendre, sems = refs
    copies = [pltpu.make_async_copy(legendre_hbm.at[q], legendre[q], sems.at[q]) for q in range(STAGED)]
    for copy in copies:
        copy.start()
    for copy in copies:
        copy.wait()


def legendre_kernel(mode_ref, msg_ref, *refs):
    early, (legendre_hbm, out_hbm, late, out, late_sems, sems, rows, mixed) = refs[:STAGED], refs[STAGED:]
    legendre = [*early, *[late.at[q] for q in range(QUADS - STAGED)]]
    copies = {
        first: pltpu.make_async_copy(
            legendre_hbm.at[pl.ds(first, last - first)], late.at[pl.ds(first - STAGED, last - first)], late_sems.at[n]
        )
        for n, (first, last) in enumerate(((STAGED, CUT), (CUT, QUADS)))
    }
    for copy in copies.values():
        copy.start()
    base = lax.axis_index("lat") * SLOTS
    rows[0:MSG] = jnp.zeros((MSG, 128), F32)
    rows[MSG : (BANDS + 1) * MSG] = msg_ref[...].reshape(BANDS * MSG, 128).astype(F32)
    rows[(BANDS + 1) * MSG :] = jnp.zeros((MSG, 128), F32)
    for g in range(GROUPS + 1):

        def part(t, neighbour):
            return rows[pl.ds((1 + neighbour) * MSG + t * (GROUPS + 1) + g, BANDS, stride=MSG), :]

        mixed[pl.ds(g * NLAT, BANDS, stride=2), :] = part(1, 0) + part(3, -1)
        mixed[pl.ds(g * NLAT + 1, BANDS, stride=2), :] = part(2, 0) + part(0, 1)
    spread = mixed[...].T
    lane = lax.broadcasted_iota(jnp.int32, (16, 128), 1)
    first = lane < NLAT
    plain = [spread[:, 128 * p : 128 * p + 128] for p in range((GROUPS + 1) // 2)]
    swapped = [pltpu.roll(p, NLAT, 1) for p in plain]
    limit = jnp.where(
        first[0:1],
        16.0 * swapped[-1][0:1] + swapped[-1][1:2],
        16.0 * plain[-1][0:1] + plain[-1][1:2],
    )
    degree = lax.broadcasted_iota(jnp.int32, (16, NL), 1)
    none = jnp.zeros((16, 128), F32)
    sent = []
    for q in range(QUADS):
        g, half = divmod(q, 2)
        left = []
        for n in range(4):
            b = 4 * half + n
            mode = mode_ref[base + g * LANE_SLOTS + b]
            keep = mode.astype(F32) < limit
            own = first if n % 2 == 0 else ~first
            value = (plain if g % 2 == n % 2 else swapped)[g // 2][16 * b : 16 * b + 16]
            value = jnp.where(keep & own, value, none)
            left.append(jnp.concatenate([value, none] if n < 2 else [none, value], axis=1))
        left = jnp.concatenate(left, axis=0).astype(BF16)
        if q in copies:
            copies[q].wait()
        result = dot(left, legendre[q][...], ((1,), (0,)))
        for n in range(4):
            slot = 4 * q + n
            mode = mode_ref[base + slot]
            block = jnp.where(degree >= mode, result[16 * n : 16 * n + 16], 0.0)
            for r in range(2):
                for f in range(FIELDS):
                    at = (r * FIELDS + f) * PER_PEER
                    out[slot, r, f] = block[at : at + PER_PEER].astype(BF16)
        here = pl.ds(4 * q, 4)
        sent.append(pltpu.make_async_copy(out.at[here], out_hbm.at[here], sems.at[q]))
        sent[-1].start()
    for copy in sent:
        copy.wait()


def params(mib):
    return pltpu.CompilerParams(vmem_limit_bytes=mib * 1024 * 1024)


def in_vmem():
    return pl.BlockSpec(memory_space=pltpu.VMEM)


def hbm(*arrays):
    return [pltpu.with_memory_space_constraint(x, pltpu.HBM) for x in arrays]


def vmem(*arrays):
    return [pltpu.with_memory_space_constraint(x, pltpu.VMEM) for x in arrays]


def in_hbm():
    return pl.BlockSpec(memory_space=pltpu.HBM)


def in_smem():
    return pl.BlockSpec(memory_space=pltpu.SMEM)


def per_device(grid_cot, weights, offsets, lat_points, slot_mode, legendre):
    sent = pl.pallas_call(
        deposit_kernel,
        name="deposit",
        out_shape=pltpu.VMEM((SECTORS, LINES, WIDE), BF16),
        in_specs=[in_hbm()] * 3,
        out_specs=in_vmem(),
        scratch_shapes=[
            pltpu.VMEM(grid_cot.shape, F32),
            pltpu.VMEM(weights.shape, BF16),
            pltpu.VMEM(offsets.shape, jnp.int32),
            pltpu.SemaphoreType.DMA((3,)),
            pltpu.VMEM((6 * ROWS * LEV, COLS), F32),
            pltpu.VMEM((COLS, 6 * LANES), F32),
            pltpu.VMEM((7, COLS + 16, LANES), F32),
            pltpu.VMEM((3, WIDE, LANES), F32),
            pltpu.VMEM((WIDE, 2 * LANES), BF16),
        ],
        compiler_params=params(14),
        cost_estimate=pl.CostEstimate(flops=20_000_000, bytes_accessed=1_500_000, transcendentals=0),
    )(*hbm(grid_cot, weights, offsets))
    column_mode = slot_mode.reshape(BANDS, GROUPS, LANE_SLOTS).transpose(2, 1, 0).reshape(1, M)
    tables = pl.pallas_call(
        table_kernel,
        name="table",
        out_shape=(
            *[pltpu.VMEM((DEPTH, 2 * BLOCK), BF16)] * BLOCKS,
            pltpu.VMEM((AUX, M), F32),
        ),
        in_specs=[in_smem(), in_vmem()],
        out_specs=(in_vmem(),) * (BLOCKS + 1),
        compiler_params=params(12),
        cost_estimate=pl.CostEstimate(flops=20_000_000, bytes_accessed=4_000_000, transcendentals=0),
    )(lat_points, column_mode)
    circles = lax.all_to_all(sent, "lon", split_axis=0, concat_axis=0, tiled=True)
    message = pl.pallas_call(
        fourier_kernel,
        name="fourier",
        out_shape=pltpu.VMEM((BANDS, MSG, 128), BF16),
        in_specs=[in_vmem()] * (BLOCKS + 2),
        out_specs=in_vmem(),
        scratch_shapes=[
            pltpu.VMEM((TARGETS, 16, M), BF16),
            pltpu.VMEM((128, TARGETS * BANDS * GROUPS), BF16),
            pltpu.VMEM((BANDS * MSG, 128), F32),
        ],
        compiler_params=params(14),
        cost_estimate=pl.CostEstimate(flops=1_000_000_000, bytes_accessed=5_000_000, transcendentals=0),
    )(circles, *vmem(*tables))
    shape = (SLOTS, 2, FIELDS, PER_PEER, NL)
    message, legendre = lax.optimization_barrier((message, legendre.reshape(QUADS, 4 * NLAT, NL)))
    staged = pl.pallas_call(
        stage_kernel,
        name="stage",
        out_shape=(
            *[pltpu.VMEM((4 * NLAT, NL), BF16)] * STAGED,
        ),
        in_specs=[in_hbm()],
        out_specs=(in_vmem(),) * STAGED,
        scratch_shapes=[pltpu.SemaphoreType.DMA((STAGED,))],
        compiler_params=params(12),
        cost_estimate=pl.CostEstimate(flops=0, bytes_accessed=16_000_000, transcendentals=0),
    )(*hbm(legendre))
    coefficients = lax.all_to_all(message, "lat", split_axis=0, concat_axis=0, tiled=True)
    return pl.pallas_call(
        legendre_kernel,
        name="legendre",
        out_shape=jax.ShapeDtypeStruct(shape, BF16),
        in_specs=[in_smem()] + [in_vmem()] * (STAGED + 1) + [in_hbm()],
        out_specs=in_hbm(),
        scratch_shapes=[
            pltpu.VMEM((QUADS - STAGED, 4 * NLAT, NL), BF16),
            pltpu.VMEM(shape, BF16),
            pltpu.SemaphoreType.DMA((2,)),
            pltpu.SemaphoreType.DMA((QUADS,)),
            pltpu.VMEM(((BANDS + 2) * MSG, 128), F32),
            pltpu.VMEM(((GROUPS + 1) * NLAT, 128), F32),
        ],
        compiler_params=params(12),
        cost_estimate=pl.CostEstimate(flops=500_000_000, bytes_accessed=8_000_000, transcendentals=0),
    )(slot_mode, coefficients, *vmem(*staged), *hbm(legendre))


def solution(mesh):
    placed = (
        P(None, "lat", None, "lon"),
        P("lat", None, None, "lon"),
        P("lat", None, None, "lon"),
        P("lat"),
        P(),
        P("lat", None, None),
    )
    return jax.shard_map(
        per_device,
        mesh=mesh,
        in_specs=placed,
        out_specs=P("lat", None, None, "lon", None),
        check_vma=False,
    )
```

```python
import functools

import jax
import jax.numpy as jnp
import numpy as np
from jax import lax
from jax.experimental import pallas as pl
from jax.experimental.pallas import tpu as pltpu
from jax.sharding import PartitionSpec as P

FIELDS = 4
NLON = 5120
M = 1280
NL = 1280
REACH = 4
LEV = 16
ROWS = 2
TARGETS = ROWS + 2
SECTORS = 8
BANDS = 32
COLS = NLON // SECTORS
WIDE = 768
PER_PEER = LEV // SECTORS
LINES = TARGETS * FIELDS * PER_PEER
SLOTS = M // BANDS
LANE_SLOTS = 8
GROUPS = SLOTS // LANE_SLOTS
MSG = TARGETS * (GROUPS + 1)
NLAT = ROWS * BANDS

F32 = jnp.float32
BF16 = jnp.bfloat16


def dot(a, b, dims):
    return lax.dot_general(a, b, (dims, ((), ())), preferred_element_type=F32)


def one_hot(target, rows):
    row = lax.broadcasted_iota(jnp.int32, (rows, target.shape[1]), 0)
    return jnp.where(row == target, 1.0, 0.0).astype(BF16)


def spread_order():
    lane = lax.broadcasted_iota(jnp.int32, (1, 6 * LANES), 1)
    kind = lane // LANES
    place = (lane // (FIELDS * LEV)) % ROWS * LEV + lane % LEV
    return one_hot(jnp.where(kind < 4, place * 4 + kind, ROWS * LEV * 4 + place * 2 + kind - 4), 6 * ROWS * LEV)


def line_order():
    lane = lax.broadcasted_iota(jnp.int32, (1, 2 * LANES), 1)
    half = lane // (FIELDS * LEV) % 2
    target = jnp.where(lane < LANES, half * 3, half + 1)
    field = lane // LEV % FIELDS
    level = lane % LEV
    row = ((level // PER_PEER * TARGETS + target) * FIELDS + field) * PER_PEER + level % PER_PEER
    return one_hot(row, SECTORS * LINES)


UNROLL = 128
LANES = FIELDS * ROWS * LEV


def deposit_kernel(
    grid_hbm, weight_hbm, offset_hbm, out_ref, grid, weight, offset, sems, stacked, wide, terms, sums, parts
):
    pairs = ((offset_hbm, offset), (weight_hbm, weight), (grid_hbm, grid))
    copies = [pltpu.make_async_copy(src, dst, sems.at[n]) for n, (src, dst) in enumerate(pairs)]
    for copy in copies:
        copy.start()
    spread = spread_order()
    order = line_order()
    for n in range(7):
        fill = jnp.full((8, LANES), 99.0 if n == 0 else 0.0, F32)
        terms[n, 0:8] = fill
        terms[n, COLS + 8 : COLS + 16] = fill
    copies[0].wait()
    for i in range(ROWS):
        for v in range(LEV):
            at = ROWS * LEV * 4 + (i * LEV + v) * 2
            stacked[at : at + 2, :] = offset[i, v].astype(F32)
    copies[1].wait()
    for i in range(ROWS):
        for v in range(LEV):
            at = (i * LEV + v) * 4
            stacked[at : at + 4, :] = weight[i, v].astype(F32)
    wide[...] = dot(stacked[...].astype(BF16), spread, ((0,), (0,)))
    copies[2].wait()
    for j in range(COLS // 128):
        rows = slice(128 * j, 128 * j + 128)
        lines = slice(128 * j + 8, 128 * j + 136)
        g = jnp.concatenate([grid[:, i, :, rows].reshape(FIELDS * LEV, 128) for i in range(ROWS)], axis=0).T
        w = [g * wide[rows, c * LANES : (c + 1) * LANES] for c in range(4)]
        south = wide[rows, 4 * LANES : 5 * LANES] < -0.5
        terms[0, lines] = wide[rows, 5 * LANES :]
        for q in range(2):
            terms[1 + q, lines] = jnp.where(south, w[q], 0.0)
            terms[3 + q, lines] = jnp.where(south, w[2 + q], w[q])
            terms[5 + q, lines] = jnp.where(south, 0.0, w[2 + q])

    def tile(start):
        total = [jnp.zeros((8, LANES), F32) for _ in range(3)]
        for n in range(2 * REACH + 1):
            shift = REACH - n
            east = terms[0, pl.ds(start + n, 8), :]
            here = east == float(shift)
            before = east == float(shift - 1)
            for r in range(3):
                first = terms[1 + 2 * r, pl.ds(start + n, 8), :]
                second = terms[2 + 2 * r, pl.ds(start + n, 8), :]
                total[r] = total[r] + jnp.where(here, first, jnp.where(before, second, 0.0))
        return total

    def step(n, carry):
        start = pl.multiple_of(n * UNROLL, UNROLL)
        for m in range(0, UNROLL, 8):
            for r, total in enumerate(tile(start + m)):
                sums[r, pl.ds(start + m, 8), :] = total
        return carry

    lax.fori_loop(0, COLS // UNROLL, step, 0)
    for r, total in enumerate(tile(COLS)):
        sums[r, COLS : COLS + 8] = total
        sums[r, COLS + 8 :] = jnp.zeros((WIDE - COLS - 8, LANES), F32)
    north, same, south = sums[0], sums[1], sums[2]
    inner = lax.broadcasted_iota(jnp.int32, (1, LANES), 1) < FIELDS * LEV
    parts[:, :LANES] = jnp.where(inner, north, south).astype(BF16)
    parts[:, LANES:] = (same + pltpu.roll(jnp.where(inner, south, north), FIELDS * LEV, 1)).astype(BF16)
    ordered = dot(order, parts[...], ((1,), (1,)))
    out_ref[...] = ordered.astype(BF16).reshape(out_ref.shape)


def sincos(count):
    turn = count - NLON * jnp.round(count * (1.0 / NLON))
    quarter = jnp.round(turn * (4.0 / NLON))
    x = (turn - (NLON // 4) * quarter) * np.float32(2.0 * np.pi / NLON)
    y = x * x
    s = x * (1.0 + y * (-1.0 / 6 + y * (1.0 / 120 + y * (-1.0 / 5040 + y * (1.0 / 362880)))))
    c = 1.0 + y * (-1.0 / 2 + y * (1.0 / 24 + y * (-1.0 / 720 + y * (1.0 / 40320))))
    odd = jnp.abs(quarter) == 1.0
    cosine = jnp.where(odd, s, c)
    sine = jnp.where(odd, c, s)
    cosine = jnp.where((quarter == 1.0) | (jnp.abs(quarter) == 2.0), -cosine, cosine)
    sine = jnp.where((quarter == -1.0) | (jnp.abs(quarter) == 2.0), -sine, sine)
    return cosine, sine


STEP = 32
HALVES = 2
DEPTH = WIDE // HALVES
TURNS = HALVES * SECTORS
BLOCK = 256
BLOCKS = M // BLOCK
AUX = 2 * TURNS + 8


def table_kernel(points_ref, mode_ref, *refs):
    *table, aux = refs
    mode = mode_ref[...].astype(F32)

    def rows(count, position):
        place = position(lax.broadcasted_iota(jnp.int32, (count, M), 0))
        return sincos(place.astype(F32) * mode)

    coarse_c, coarse_s = rows(DEPTH // STEP, lambda n: n * STEP)
    fine_c, fine_s = rows(STEP, lambda n: n - REACH)
    factor = jnp.where(mode == 0.0, 1.0, 2.0)
    fine_c = fine_c * factor
    fine_s = fine_s * factor
    for n in range(BLOCKS):
        part = slice(n * BLOCK, (n + 1) * BLOCK)
        for a in range(DEPTH // STEP):
            c = coarse_c[a : a + 1, part]
            s = coarse_s[a : a + 1, part]
            lines = slice(a * STEP, (a + 1) * STEP)
            table[n][lines, :BLOCK] = (c * fine_c[:, part] - s * fine_s[:, part]).astype(BF16)
            table[n][lines, BLOCK:] = (-s * fine_c[:, part] - c * fine_s[:, part]).astype(BF16)
    turn_c, turn_s = rows(TURNS, lambda n: n % SECTORS * COLS + n // SECTORS * DEPTH)
    aux[0:TURNS, :] = turn_c
    aux[TURNS : 2 * TURNS, :] = turn_s
    row = lax.broadcasted_iota(jnp.int32, (AUX - 2 * TURNS, M), 0)
    lane = lax.broadcasted_iota(jnp.int32, (AUX - 2 * TURNS, M), 1)
    extra = jnp.zeros((AUX - 2 * TURNS, M), F32)
    for i in range(ROWS):
        count = (points_ref[i] + 1) // 2
        high = count // 16
        value = jnp.where(lane == 0, high, jnp.where(lane == 1, count - 16 * high, 0))
        extra = extra + jnp.where(row == i, value, 0).astype(F32)
    aux[2 * TURNS :, :] = extra


def fourier_kernel(grid_ref, *refs):
    *table, aux, out_ref, spectra, lanes, rows = refs
    data = [grid_ref[:, :, h * DEPTH : (h + 1) * DEPTH].reshape(SECTORS * LINES, DEPTH) for h in range(HALVES)]
    for n in range(BLOCKS):
        part = slice(n * BLOCK, (n + 1) * BLOCK)
        sum_r = jnp.zeros((LINES, BLOCK), F32)
        sum_i = jnp.zeros((LINES, BLOCK), F32)
        for h in range(HALVES):
            real = dot(data[h], table[n][:, :BLOCK], ((1,), (0,)))
            imag = dot(data[h], table[n][:, BLOCK:], ((1,), (0,)))
            for j in range(SECTORS):
                turn = h * SECTORS + j
                c = aux[turn : turn + 1, part]
                s = aux[TURNS + turn : TURNS + turn + 1, part]
                re = real[j * LINES : (j + 1) * LINES]
                im = imag[j * LINES : (j + 1) * LINES]
                sum_r = sum_r + c * re + s * im
                sum_i = sum_i + c * im - s * re
        for t in range(TARGETS):
            here = slice(8 * t, 8 * t + 8)
            spectra[t, :, part] = jnp.concatenate([sum_r[here], sum_i[here]], axis=0).astype(BF16)
    run = BANDS * GROUPS
    for t in range(TARGETS):
        for b in range(LANE_SLOTS):
            lanes[16 * b : 16 * b + 16, t * run : (t + 1) * run] = spectra[t, :, b * run : (b + 1) * run]
    turned = lanes[...].astype(F32).T
    for t in range(TARGETS):
        for g in range(GROUPS):
            at = (t * GROUPS + g) * BANDS
            rows[pl.ds(t * (GROUPS + 1) + g, BANDS, stride=MSG), :] = turned[at : at + BANDS]
        limit = jnp.zeros((BANDS, 128), F32)
        if 0 < t <= ROWS:
            limit = limit + aux[2 * TURNS + t - 1 : 2 * TURNS + t, 0:128]
        rows[pl.ds(t * (GROUPS + 1) + GROUPS, BANDS, stride=MSG), :] = limit
    out_ref[...] = rows[: BANDS * MSG].astype(BF16).reshape(out_ref.shape)


QUADS = SLOTS // 4
STAGED = 5
CUT = 8


def stage_kernel(legendre_hbm, *refs):
    *legendre, sems = refs
    copies = [pltpu.make_async_copy(legendre_hbm.at[q], legendre[q], sems.at[q]) for q in range(STAGED)]
    for copy in copies:
        copy.start()
    for copy in copies:
        copy.wait()


def legendre_kernel(mode_ref, msg_ref, *refs):
    early, (legendre_hbm, out_hbm, late, out, late_sems, sems, rows, mixed) = refs[:STAGED], refs[STAGED:]
    legendre = [*early, *[late.at[q] for q in range(QUADS - STAGED)]]
    copies = {
        first: pltpu.make_async_copy(
            legendre_hbm.at[pl.ds(first, last - first)], late.at[pl.ds(first - STAGED, last - first)], late_sems.at[n]
        )
        for n, (first, last) in enumerate(((STAGED, CUT), (CUT, QUADS)))
    }
    for copy in copies.values():
        copy.start()
    base = lax.axis_index("lat") * SLOTS
    rows[0:MSG] = jnp.zeros((MSG, 128), F32)
    rows[MSG : (BANDS + 1) * MSG] = msg_ref[...].reshape(BANDS * MSG, 128).astype(F32)
    rows[(BANDS + 1) * MSG :] = jnp.zeros((2 * MSG, 128), F32)
    for g in range(GROUPS + 1):

        def part(t, neighbour):
            return rows[pl.ds((1 + neighbour) * MSG + t * (GROUPS + 1) + g, BANDS, stride=MSG), :]

        mixed[pl.ds(g * NLAT, BANDS, stride=2), :] = part(1, 0) + part(3, -1)
        mixed[pl.ds(g * NLAT + 1, BANDS, stride=2), :] = part(2, 0) + part(0, 1)
    spread = mixed[: (GROUPS + 1) * NLAT].T
    lane = lax.broadcasted_iota(jnp.int32, (16, 128), 1)
    first = lane < NLAT
    plain = [spread[:, 128 * p : 128 * p + 128] for p in range((GROUPS + 1) // 2)]
    swapped = [pltpu.roll(p, NLAT, 1) for p in plain]
    limit = jnp.where(
        first[0:1],
        16.0 * swapped[-1][0:1] + swapped[-1][1:2],
        16.0 * plain[-1][0:1] + plain[-1][1:2],
    )
    degree = lax.broadcasted_iota(jnp.int32, (16, NL), 1)
    none = jnp.zeros((16, 128), F32)
    sent = []
    for q in range(QUADS):
        g, half = divmod(q, 2)
        left = []
        for n in range(4):
            b = 4 * half + n
            mode = mode_ref[base + g * LANE_SLOTS + b]
            keep = mode.astype(F32) < limit
            own = first if n % 2 == 0 else ~first
            value = (plain if g % 2 == n % 2 else swapped)[g // 2][16 * b : 16 * b + 16]
            value = jnp.where(keep & own, value, none)
            left.append(jnp.concatenate([value, none] if n < 2 else [none, value], axis=1))
        left = jnp.concatenate(left, axis=0).astype(BF16)
        if q in copies:
            copies[q].wait()
        result = dot(left, legendre[q][...], ((1,), (0,)))
        for n in range(4):
            slot = 4 * q + n
            mode = mode_ref[base + slot]
            block = jnp.where(degree >= mode, result[16 * n : 16 * n + 16], 0.0)
            for r in range(2):
                for f in range(FIELDS):
                    at = (r * FIELDS + f) * PER_PEER
                    out[slot, r, f] = block[at : at + PER_PEER].astype(BF16)
        here = pl.ds(4 * q, 4)
        sent.append(pltpu.make_async_copy(out.at[here], out_hbm.at[here], sems.at[q]))
        sent[-1].start()
    for copy in sent:
        copy.wait()


def params(mib):
    return pltpu.CompilerParams(vmem_limit_bytes=mib * 1024 * 1024)


def in_vmem():
    return pl.BlockSpec(memory_space=pltpu.VMEM)


def hbm(*arrays):
    return [pltpu.with_memory_space_constraint(x, pltpu.HBM) for x in arrays]


def vmem(*arrays):
    return [pltpu.with_memory_space_constraint(x, pltpu.VMEM) for x in arrays]


def in_hbm():
    return pl.BlockSpec(memory_space=pltpu.HBM)


def in_smem():
    return pl.BlockSpec(memory_space=pltpu.SMEM)


def per_device(grid_cot, weights, offsets, lat_points, slot_mode, legendre):
    sent = pl.pallas_call(
        deposit_kernel,
        name="deposit",
        out_shape=pltpu.VMEM((SECTORS, LINES, WIDE), BF16),
        in_specs=[in_hbm()] * 3,
        out_specs=in_vmem(),
        scratch_shapes=[
            pltpu.VMEM(grid_cot.shape, F32),
            pltpu.VMEM(weights.shape, BF16),
            pltpu.VMEM(offsets.shape, jnp.int32),
            pltpu.SemaphoreType.DMA((3,)),
            pltpu.VMEM((6 * ROWS * LEV, COLS), F32),
            pltpu.VMEM((COLS, 6 * LANES), F32),
            pltpu.VMEM((7, COLS + 16, LANES), F32),
            pltpu.VMEM((3, WIDE, LANES), F32),
            pltpu.VMEM((WIDE, 2 * LANES), BF16),
        ],
        compiler_params=params(14),
        cost_estimate=pl.CostEstimate(flops=20_000_000, bytes_accessed=1_500_000, transcendentals=0),
    )(*hbm(grid_cot, weights, offsets))
    column_mode = slot_mode.reshape(BANDS, GROUPS, LANE_SLOTS).transpose(2, 1, 0).reshape(1, M)
    tables = pl.pallas_call(
        table_kernel,
        name="table",
        out_shape=(
            *[pltpu.VMEM((DEPTH, 2 * BLOCK), BF16)] * BLOCKS,
            pltpu.VMEM((AUX, M), F32),
        ),
        in_specs=[in_smem(), in_vmem()],
        out_specs=(in_vmem(),) * (BLOCKS + 1),
        compiler_params=params(12),
        cost_estimate=pl.CostEstimate(flops=20_000_000, bytes_accessed=4_000_000, transcendentals=0),
    )(lat_points, column_mode)
    circles = lax.all_to_all(sent, "lon", split_axis=0, concat_axis=0, tiled=True)
    message = pl.pallas_call(
        fourier_kernel,
        name="fourier",
        out_shape=pltpu.VMEM((BANDS, MSG, 128), BF16),
        in_specs=[in_vmem()] * (BLOCKS + 2),
        out_specs=in_vmem(),
        scratch_shapes=[
            pltpu.VMEM((TARGETS, 16, M), BF16),
            pltpu.VMEM((128, TARGETS * BANDS * GROUPS), BF16),
            pltpu.VMEM(((BANDS + 1) * MSG, 128), F32),
        ],
        compiler_params=params(14),
        cost_estimate=pl.CostEstimate(flops=1_000_000_000, bytes_accessed=5_000_000, transcendentals=0),
    )(circles, *vmem(*tables))
    shape = (SLOTS, 2, FIELDS, PER_PEER, NL)
    message, legendre = lax.optimization_barrier((message, legendre.reshape(QUADS, 4 * NLAT, NL)))
    staged = pl.pallas_call(
        stage_kernel,
        name="stage",
        out_shape=(
            *[pltpu.VMEM((4 * NLAT, NL), BF16)] * STAGED,
        ),
        in_specs=[in_hbm()],
        out_specs=(in_vmem(),) * STAGED,
        scratch_shapes=[pltpu.SemaphoreType.DMA((STAGED,))],
        compiler_params=params(12),
        cost_estimate=pl.CostEstimate(flops=0, bytes_accessed=16_000_000, transcendentals=0),
    )(*hbm(legendre))
    coefficients = lax.all_to_all(message, "lat", split_axis=0, concat_axis=0, tiled=True)
    return pl.pallas_call(
        legendre_kernel,
        name="legendre",
        out_shape=jax.ShapeDtypeStruct(shape, BF16),
        in_specs=[in_smem()] + [in_vmem()] * (STAGED + 1) + [in_hbm()],
        out_specs=in_hbm(),
        scratch_shapes=[
            pltpu.VMEM((QUADS - STAGED, 4 * NLAT, NL), BF16),
            pltpu.VMEM(shape, BF16),
            pltpu.SemaphoreType.DMA((2,)),
            pltpu.SemaphoreType.DMA((QUADS,)),
            pltpu.VMEM(((BANDS + 3) * MSG, 128), F32),
            pltpu.VMEM(((GROUPS + 1) * NLAT + 8, 128), F32),
        ],
        compiler_params=params(12),
        cost_estimate=pl.CostEstimate(flops=500_000_000, bytes_accessed=8_000_000, transcendentals=0),
    )(slot_mode, coefficients, *vmem(*staged), *hbm(legendre))


def solution(mesh):
    placed = (
        P(None, "lat", None, "lon"),
        P("lat", None, None, "lon"),
        P("lat", None, None, "lon"),
        P("lat"),
        P(),
        P("lat", None, None),
    )
    return jax.shard_map(
        per_device,
        mesh=mesh,
        in_specs=placed,
        out_specs=P("lat", None, None, "lon", None),
        check_vma=False,
    )
```

```python
import functools

import jax
import jax.numpy as jnp
import numpy as np
from jax import lax
from jax.experimental import pallas as pl
from jax.experimental.pallas import tpu as pltpu
from jax.sharding import PartitionSpec as P

FIELDS = 4
NLON = 5120
M = 1280
NL = 1280
REACH = 4
LEV = 16
ROWS = 2
TARGETS = ROWS + 2
SECTORS = 8
BANDS = 32
COLS = NLON // SECTORS
WIDE = 768
PER_PEER = LEV // SECTORS
LINES = TARGETS * FIELDS * PER_PEER
SLOTS = M // BANDS
LANE_SLOTS = 8
GROUPS = SLOTS // LANE_SLOTS
MSG = TARGETS * (GROUPS + 1)
NLAT = ROWS * BANDS

F32 = jnp.float32
BF16 = jnp.bfloat16


def dot(a, b, dims):
    return lax.dot_general(a, b, (dims, ((), ())), preferred_element_type=F32)


def one_hot(target, rows):
    row = lax.broadcasted_iota(jnp.int32, (rows, target.shape[1]), 0)
    return jnp.where(row == target, 1.0, 0.0).astype(BF16)


def spread_order():
    lane = lax.broadcasted_iota(jnp.int32, (1, 6 * LANES), 1)
    kind = lane // LANES
    place = (lane // (FIELDS * LEV)) % ROWS * LEV + lane % LEV
    return one_hot(jnp.where(kind < 4, place * 4 + kind, ROWS * LEV * 4 + place * 2 + kind - 4), 6 * ROWS * LEV)


def line_order():
    lane = lax.broadcasted_iota(jnp.int32, (1, 2 * LANES), 1)
    half = lane // (FIELDS * LEV) % 2
    target = jnp.where(lane < LANES, half * 3, half + 1)
    field = lane // LEV % FIELDS
    level = lane % LEV
    row = ((level // PER_PEER * TARGETS + target) * FIELDS + field) * PER_PEER + level % PER_PEER
    return one_hot(row, SECTORS * LINES)


UNROLL = 128
LANES = FIELDS * ROWS * LEV


def deposit_kernel(
    grid_hbm, weight_hbm, offset_hbm, out_ref, grid, weight, offset, sems, stacked, wide, terms, sums, parts, spread, order
):
    pairs = ((offset_hbm, offset), (weight_hbm, weight), (grid_hbm, grid))
    copies = [pltpu.make_async_copy(src, dst, sems.at[n]) for n, (src, dst) in enumerate(pairs)]
    for copy in copies:
        copy.start()

    @pl.when(lax.axis_index("lat") >= 0)
    def _():
        spread[...] = spread_order()
        order[...] = line_order()
        for n in range(7):
            fill = jnp.full((8, LANES), 99.0 if n == 0 else 0.0, F32)
            terms[n, 0:8] = fill
            terms[n, COLS + 8 : COLS + 16] = fill

    copies[0].wait()
    for i in range(ROWS):
        for v in range(LEV):
            at = ROWS * LEV * 4 + (i * LEV + v) * 2
            stacked[at : at + 2, :] = offset[i, v].astype(F32)
    copies[1].wait()
    for i in range(ROWS):
        for v in range(LEV):
            at = (i * LEV + v) * 4
            stacked[at : at + 4, :] = weight[i, v].astype(F32)
    wide[...] = dot(stacked[...].astype(BF16), spread[...], ((0,), (0,)))
    copies[2].wait()
    for j in range(COLS // 128):
        rows = slice(128 * j, 128 * j + 128)
        lines = slice(128 * j + 8, 128 * j + 136)
        g = jnp.concatenate([grid[:, i, :, rows].reshape(FIELDS * LEV, 128) for i in range(ROWS)], axis=0).T
        w = [g * wide[rows, c * LANES : (c + 1) * LANES] for c in range(4)]
        south = wide[rows, 4 * LANES : 5 * LANES] < -0.5
        terms[0, lines] = wide[rows, 5 * LANES :]
        for q in range(2):
            terms[1 + q, lines] = jnp.where(south, w[q], 0.0)
            terms[3 + q, lines] = jnp.where(south, w[2 + q], w[q])
            terms[5 + q, lines] = jnp.where(south, 0.0, w[2 + q])

    def tile(start):
        total = [jnp.zeros((8, LANES), F32) for _ in range(3)]
        for n in range(2 * REACH + 1):
            shift = REACH - n
            east = terms[0, pl.ds(start + n, 8), :]
            here = east == float(shift)
            before = east == float(shift - 1)
            for r in range(3):
                first = terms[1 + 2 * r, pl.ds(start + n, 8), :]
                second = terms[2 + 2 * r, pl.ds(start + n, 8), :]
                total[r] = total[r] + jnp.where(here, first, jnp.where(before, second, 0.0))
        return total

    def step(n, carry):
        start = pl.multiple_of(n * UNROLL, UNROLL)
        for m in range(0, UNROLL, 8):
            for r, total in enumerate(tile(start + m)):
                sums[r, pl.ds(start + m, 8), :] = total
        return carry

    lax.fori_loop(0, COLS // UNROLL, step, 0)
    for r, total in enumerate(tile(COLS)):
        sums[r, COLS : COLS + 8] = total
        sums[r, COLS + 8 :] = jnp.zeros((WIDE - COLS - 8, LANES), F32)
    north, same, south = sums[0], sums[1], sums[2]
    inner = lax.broadcasted_iota(jnp.int32, (1, LANES), 1) < FIELDS * LEV
    parts[:, :LANES] = jnp.where(inner, north, south).astype(BF16)
    parts[:, LANES:] = (same + pltpu.roll(jnp.where(inner, south, north), FIELDS * LEV, 1)).astype(BF16)
    ordered = dot(order[...], parts[...], ((1,), (1,)))
    out_ref[...] = ordered.astype(BF16).reshape(out_ref.shape)


def sincos(count):
    turn = count - NLON * jnp.round(count * (1.0 / NLON))
    quarter = jnp.round(turn * (4.0 / NLON))
    x = (turn - (NLON // 4) * quarter) * np.float32(2.0 * np.pi / NLON)
    y = x * x
    s = x * (1.0 + y * (-1.0 / 6 + y * (1.0 / 120 + y * (-1.0 / 5040 + y * (1.0 / 362880)))))
    c = 1.0 + y * (-1.0 / 2 + y * (1.0 / 24 + y * (-1.0 / 720 + y * (1.0 / 40320))))
    odd = jnp.abs(quarter) == 1.0
    cosine = jnp.where(odd, s, c)
    sine = jnp.where(odd, c, s)
    cosine = jnp.where((quarter == 1.0) | (jnp.abs(quarter) == 2.0), -cosine, cosine)
    sine = jnp.where((quarter == -1.0) | (jnp.abs(quarter) == 2.0), -sine, sine)
    return cosine, sine


STEP = 32
HALVES = 2
DEPTH = WIDE // HALVES
TURNS = HALVES * SECTORS
BLOCK = 256
BLOCKS = M // BLOCK
AUX = 2 * TURNS + 8


def table_kernel(points_ref, mode_ref, *refs):
    *table, aux = refs
    mode = mode_ref[...].astype(F32)

    def rows(count, position):
        place = position(lax.broadcasted_iota(jnp.int32, (count, M), 0))
        return sincos(place.astype(F32) * mode)

    coarse_c, coarse_s = rows(DEPTH // STEP, lambda n: n * STEP)
    fine_c, fine_s = rows(STEP, lambda n: n - REACH)
    factor = jnp.where(mode == 0.0, 1.0, 2.0)
    fine_c = fine_c * factor
    fine_s = fine_s * factor
    for n in range(BLOCKS):
        part = slice(n * BLOCK, (n + 1) * BLOCK)
        for a in range(DEPTH // STEP):
            c = coarse_c[a : a + 1, part]
            s = coarse_s[a : a + 1, part]
            lines = slice(a * STEP, (a + 1) * STEP)
            table[n][lines, :BLOCK] = (c * fine_c[:, part] - s * fine_s[:, part]).astype(BF16)
            table[n][lines, BLOCK:] = (-s * fine_c[:, part] - c * fine_s[:, part]).astype(BF16)
    turn_c, turn_s = rows(TURNS, lambda n: n % SECTORS * COLS + n // SECTORS * DEPTH)
    aux[0:TURNS, :] = turn_c
    aux[TURNS : 2 * TURNS, :] = turn_s
    row = lax.broadcasted_iota(jnp.int32, (AUX - 2 * TURNS, M), 0)
    lane = lax.broadcasted_iota(jnp.int32, (AUX - 2 * TURNS, M), 1)
    extra = jnp.zeros((AUX - 2 * TURNS, M), F32)
    for i in range(ROWS):
        count = (points_ref[i] + 1) // 2
        high = count // 16
        value = jnp.where(lane == 0, high, jnp.where(lane == 1, count - 16 * high, 0))
        extra = extra + jnp.where(row == i, value, 0).astype(F32)
    aux[2 * TURNS :, :] = extra


def fourier_kernel(grid_ref, *refs):
    *table, aux, out_ref, spectra, lanes, rows = refs
    data = [grid_ref[:, :, h * DEPTH : (h + 1) * DEPTH].reshape(SECTORS * LINES, DEPTH) for h in range(HALVES)]
    for n in range(BLOCKS):
        part = slice(n * BLOCK, (n + 1) * BLOCK)
        sum_r = jnp.zeros((LINES, BLOCK), F32)
        sum_i = jnp.zeros((LINES, BLOCK), F32)
        for h in range(HALVES):
            real = dot(data[h], table[n][:, :BLOCK], ((1,), (0,)))
            imag = dot(data[h], table[n][:, BLOCK:], ((1,), (0,)))
            for j in range(SECTORS):
                turn = h * SECTORS + j
                c = aux[turn : turn + 1, part]
                s = aux[TURNS + turn : TURNS + turn + 1, part]
                re = real[j * LINES : (j + 1) * LINES]
                im = imag[j * LINES : (j + 1) * LINES]
                sum_r = sum_r + c * re + s * im
                sum_i = sum_i + c * im - s * re
        for t in range(TARGETS):
            here = slice(8 * t, 8 * t + 8)
            spectra[t, :, part] = jnp.concatenate([sum_r[here], sum_i[here]], axis=0).astype(BF16)
    run = BANDS * GROUPS
    for t in range(TARGETS):
        for b in range(LANE_SLOTS):
            lanes[16 * b : 16 * b + 16, t * run : (t + 1) * run] = spectra[t, :, b * run : (b + 1) * run]
    turned = lanes[...].astype(F32).T
    for t in range(TARGETS):
        for g in range(GROUPS):
            at = (t * GROUPS + g) * BANDS
            rows[pl.ds(t * (GROUPS + 1) + g, BANDS, stride=MSG), :] = turned[at : at + BANDS]
        limit = jnp.zeros((BANDS, 128), F32)
        if 0 < t <= ROWS:
            limit = limit + aux[2 * TURNS + t - 1 : 2 * TURNS + t, 0:128]
        rows[pl.ds(t * (GROUPS + 1) + GROUPS, BANDS, stride=MSG), :] = limit
    out_ref[...] = rows[: BANDS * MSG].astype(BF16).reshape(out_ref.shape)


QUADS = SLOTS // 4
STAGED = 5
CUT = 8


def stage_kernel(legendre_hbm, *refs):
    *legendre, sems = refs
    copies = [pltpu.make_async_copy(legendre_hbm.at[q], legendre[q], sems.at[q]) for q in range(STAGED)]
    for copy in copies:
        copy.start()
    for copy in copies:
        copy.wait()


def legendre_kernel(mode_ref, msg_ref, *refs):
    early, (legendre_hbm, out_hbm, late, out, late_sems, sems, rows, mixed) = refs[:STAGED], refs[STAGED:]
    legendre = [*early, *[late.at[q] for q in range(QUADS - STAGED)]]
    copies = {
        first: pltpu.make_async_copy(
            legendre_hbm.at[pl.ds(first, last - first)], late.at[pl.ds(first - STAGED, last - first)], late_sems.at[n]
        )
        for n, (first, last) in enumerate(((STAGED, CUT), (CUT, QUADS)))
    }
    for copy in copies.values():
        copy.start()
    base = lax.axis_index("lat") * SLOTS
    rows[0:MSG] = jnp.zeros((MSG, 128), F32)
    rows[MSG : (BANDS + 1) * MSG] = msg_ref[...].reshape(BANDS * MSG, 128).astype(F32)
    rows[(BANDS + 1) * MSG :] = jnp.zeros((2 * MSG, 128), F32)
    for g in range(GROUPS + 1):

        def part(t, neighbour):
            return rows[pl.ds((1 + neighbour) * MSG + t * (GROUPS + 1) + g, BANDS, stride=MSG), :]

        mixed[pl.ds(g * NLAT, BANDS, stride=2), :] = part(1, 0) + part(3, -1)
        mixed[pl.ds(g * NLAT + 1, BANDS, stride=2), :] = part(2, 0) + part(0, 1)
    spread = mixed[: (GROUPS + 1) * NLAT].T
    lane = lax.broadcasted_iota(jnp.int32, (16, 128), 1)
    first = lane < NLAT
    plain = [spread[:, 128 * p : 128 * p + 128] for p in range((GROUPS + 1) // 2)]
    swapped = [pltpu.roll(p, NLAT, 1) for p in plain]
    limit = jnp.where(
        first[0:1],
        16.0 * swapped[-1][0:1] + swapped[-1][1:2],
        16.0 * plain[-1][0:1] + plain[-1][1:2],
    )
    degree = lax.broadcasted_iota(jnp.int32, (16, NL), 1)
    none = jnp.zeros((16, 128), F32)
    sent = []
    for q in range(QUADS):
        g, half = divmod(q, 2)
        left = []
        for n in range(4):
            b = 4 * half + n
            mode = mode_ref[base + g * LANE_SLOTS + b]
            keep = mode.astype(F32) < limit
            own = first if n % 2 == 0 else ~first
            value = (plain if g % 2 == n % 2 else swapped)[g // 2][16 * b : 16 * b + 16]
            value = jnp.where(keep & own, value, none)
            left.append(jnp.concatenate([value, none] if n < 2 else [none, value], axis=1))
        left = jnp.concatenate(left, axis=0).astype(BF16)
        if q in copies:
            copies[q].wait()
        result = dot(left, legendre[q][...], ((1,), (0,)))
        for n in range(4):
            slot = 4 * q + n
            mode = mode_ref[base + slot]
            block = jnp.where(degree >= mode, result[16 * n : 16 * n + 16], 0.0)
            for r in range(2):
                for f in range(FIELDS):
                    at = (r * FIELDS + f) * PER_PEER
                    out[slot, r, f] = block[at : at + PER_PEER].astype(BF16)
        here = pl.ds(4 * q, 4)
        sent.append(pltpu.make_async_copy(out.at[here], out_hbm.at[here], sems.at[q]))
        sent[-1].start()
    for copy in sent:
        copy.wait()


def params(mib):
    return pltpu.CompilerParams(vmem_limit_bytes=mib * 1024 * 1024)


def in_vmem():
    return pl.BlockSpec(memory_space=pltpu.VMEM)


def hbm(*arrays):
    return [pltpu.with_memory_space_constraint(x, pltpu.HBM) for x in arrays]


def vmem(*arrays):
    return [pltpu.with_memory_space_constraint(x, pltpu.VMEM) for x in arrays]


def in_hbm():
    return pl.BlockSpec(memory_space=pltpu.HBM)


def in_smem():
    return pl.BlockSpec(memory_space=pltpu.SMEM)


def per_device(grid_cot, weights, offsets, lat_points, slot_mode, legendre):
    sent = pl.pallas_call(
        deposit_kernel,
        name="deposit",
        out_shape=pltpu.VMEM((SECTORS, LINES, WIDE), BF16),
        in_specs=[in_hbm()] * 3,
        out_specs=in_vmem(),
        scratch_shapes=[
            pltpu.VMEM(grid_cot.shape, F32),
            pltpu.VMEM(weights.shape, BF16),
            pltpu.VMEM(offsets.shape, jnp.int32),
            pltpu.SemaphoreType.DMA((3,)),
            pltpu.VMEM((6 * ROWS * LEV, COLS), F32),
            pltpu.VMEM((COLS, 6 * LANES), F32),
            pltpu.VMEM((7, COLS + 16, LANES), F32),
            pltpu.VMEM((3, WIDE, LANES), F32),
            pltpu.VMEM((WIDE, 2 * LANES), BF16),
            pltpu.VMEM((6 * ROWS * LEV, 6 * LANES), BF16),
            pltpu.VMEM((SECTORS * LINES, 2 * LANES), BF16),
        ],
        compiler_params=params(14),
        cost_estimate=pl.CostEstimate(flops=20_000_000, bytes_accessed=1_500_000, transcendentals=0),
    )(*hbm(grid_cot, weights, offsets))
    column_mode = slot_mode.reshape(BANDS, GROUPS, LANE_SLOTS).transpose(2, 1, 0).reshape(1, M)
    tables = pl.pallas_call(
        table_kernel,
        name="table",
        out_shape=(
            *[pltpu.VMEM((DEPTH, 2 * BLOCK), BF16)] * BLOCKS,
            pltpu.VMEM((AUX, M), F32),
        ),
        in_specs=[in_smem(), in_vmem()],
        out_specs=(in_vmem(),) * (BLOCKS + 1),
        compiler_params=params(12),
        cost_estimate=pl.CostEstimate(flops=20_000_000, bytes_accessed=4_000_000, transcendentals=0),
    )(lat_points, column_mode)
    circles = lax.all_to_all(sent, "lon", split_axis=0, concat_axis=0, tiled=True)
    message = pl.pallas_call(
        fourier_kernel,
        name="fourier",
        out_shape=pltpu.VMEM((BANDS, MSG, 128), BF16),
        in_specs=[in_vmem()] * (BLOCKS + 2),
        out_specs=in_vmem(),
        scratch_shapes=[
            pltpu.VMEM((TARGETS, 16, M), BF16),
            pltpu.VMEM((128, TARGETS * BANDS * GROUPS), BF16),
            pltpu.VMEM(((BANDS + 1) * MSG, 128), F32),
        ],
        compiler_params=params(14),
        cost_estimate=pl.CostEstimate(flops=1_000_000_000, bytes_accessed=5_000_000, transcendentals=0),
    )(circles, *vmem(*tables))
    shape = (SLOTS, 2, FIELDS, PER_PEER, NL)
    message, legendre = lax.optimization_barrier((message, legendre.reshape(QUADS, 4 * NLAT, NL)))
    staged = pl.pallas_call(
        stage_kernel,
        name="stage",
        out_shape=(
            *[pltpu.VMEM((4 * NLAT, NL), BF16)] * STAGED,
        ),
        in_specs=[in_hbm()],
        out_specs=(in_vmem(),) * STAGED,
        scratch_shapes=[pltpu.SemaphoreType.DMA((STAGED,))],
        compiler_params=params(12),
        cost_estimate=pl.CostEstimate(flops=0, bytes_accessed=16_000_000, transcendentals=0),
    )(*hbm(legendre))
    coefficients = lax.all_to_all(message, "lat", split_axis=0, concat_axis=0, tiled=True)
    return pl.pallas_call(
        legendre_kernel,
        name="legendre",
        out_shape=jax.ShapeDtypeStruct(shape, BF16),
        in_specs=[in_smem()] + [in_vmem()] * (STAGED + 1) + [in_hbm()],
        out_specs=in_hbm(),
        scratch_shapes=[
            pltpu.VMEM((QUADS - STAGED, 4 * NLAT, NL), BF16),
            pltpu.VMEM(shape, BF16),
            pltpu.SemaphoreType.DMA((2,)),
            pltpu.SemaphoreType.DMA((QUADS,)),
            pltpu.VMEM(((BANDS + 3) * MSG, 128), F32),
            pltpu.VMEM(((GROUPS + 1) * NLAT + 8, 128), F32),
        ],
        compiler_params=params(12),
        cost_estimate=pl.CostEstimate(flops=500_000_000, bytes_accessed=8_000_000, transcendentals=0),
    )(slot_mode, coefficients, *vmem(*staged), *hbm(legendre))


def solution(mesh):
    placed = (
        P(None, "lat", None, "lon"),
        P("lat", None, None, "lon"),
        P("lat", None, None, "lon"),
        P("lat"),
        P(),
        P("lat", None, None),
    )
    return jax.shard_map(
        per_device,
        mesh=mesh,
        in_specs=placed,
        out_specs=P("lat", None, None, "lon", None),
        check_vma=False,
    )
```
